256 devices in a mesh: seq: 64 (over x, z, core), sp: 4 (over y).
Axes of the slice: x: 4, y: 4, z: 8, core: 2. Of those that a mesh axis runs over, the one named last changes fastest.
Arguments:
- latents: bfloat16 [128, 32, 128], P('seq', None, 'sp'), may hold values from -6 to 6
- conv_in_weight: bfloat16 [432, 384], replicated, may hold values from -0.3125 to 0.3125
- norm_gain: float32 [384], replicated, may hold values from 0.25 to 1.75
- conv_weight: bfloat16 [10368, 384], P(None, 'sp'), may hold values from -0.0625 to 0.0625
- frame_list: int32 [64], replicated, may hold values from 0 to 127, as said below
- reward_scale: float32 [64], P('seq'), may hold values from 0.5 to 2
- patch_weight: bfloat16 [1536, 1024], replicated, may hold values from -0.15625 to 0.15625
- ln_gain: float32 [2, 1024], replicated, may hold values from 0.25 to 1.75
- qkv_weight: bfloat16 [1024, 3072], P(None, 'sp'), may hold values from -0.1875 to 0.1875
- out_weight: bfloat16 [1024, 1024], P('sp'), may hold values from -0.1875 to 0.1875
- head_vec: float32 [1024], replicated, may hold values from -1.5 to 1.5
Outputs:
- rewards: float32 [64], P('seq')
- latent_grad: float32 [128, 32, 128], P('seq', None, 'sp')
The draws below stay inside these ranges and needn't reach their ends.
Inputs may be any that keep to these rules, and one draw needn't show every extreme that they name: `frame_list`: entry j is a frame of clip j // 8, that is between (j // 8) * 16 and that plus 16 - 1; within a clip the entries are distinct and rising.
All inputs are finite; a program needn't handle non-finite values.
Results may differ from the reference program's by a relative error of at most 0.038.
Values may be sent and summed in bfloat16 or wider, within the bound.
A program may use at most 128 MiB of HBM per device.

```python
import math
import jax
import jax.numpy as jnp
from jax import lax

LAT = 16
CH = 384
VW = 1024
HEADS = 16
HD = 64
COLS = 8
CLIP_FR = 16
SEL_CLIP = 8
FRAMES = 128
HEIGHT = 32
CLIPS = 8
PICKED = 64
LAT_COLS = 128
TOKENS = 64


def draw_frame_list(key, part):
    key = jax.random.fold_in(key, 11)
    clip_keys = jax.random.split(key, CLIPS)
    picks = jax.vmap(lambda clip_key: jnp.sort(jax.random.permutation(clip_key, CLIP_FR)[:SEL_CLIP]))(clip_keys)
    starts = (jnp.arange(CLIPS, dtype=jnp.int32) * CLIP_FR)[:, None]
    return (picks.astype(jnp.int32) + starts).reshape(CLIPS * SEL_CLIP)


def level_of(rng, extent, shards, least, high):
    def one(axis_at, parts):
        draws = jax.random.uniform(jax.random.fold_in(jax.random.fold_in(rng, 6), axis_at), (parts,), jnp.float32, least / len(shards), high / len(shards))
        return jnp.repeat(jnp.exp(draws), extent[axis_at] // parts).reshape((-1,) + (1,) * (len(extent) - axis_at - 1))

    factor_of = one(*shards[0])
    for cut in shards[1:]:
        factor_of = factor_of * one(*cut)
    return factor_of


def normal_values(stream_key, extent, deviation, limit, cuts=(), kind=jnp.bfloat16):
    level = level_of(stream_key, extent, cuts, -0.22, 0.18) if cuts else 1.0
    array = jax.random.normal(stream_key, extent, jnp.float32) * deviation * level
    return jnp.minimum(jnp.maximum(array, -limit), limit).astype(kind)


def setup_inputs(seed: int = 0) -> dict:
    seeds = jax.random.split(jax.random.key(seed), 12)
    latents = normal_values(seeds[0], (FRAMES, HEIGHT, LAT_COLS), 1.0, 6.0, ((0, 64), (2, 4)))
    conv_in_weight = normal_values(seeds[1], (27 * LAT, CH), (27 * LAT) ** -0.5, 0.3125)
    norm_gain = jnp.clip(1.0 + 0.15 * jax.random.normal(seeds[2], (CH,), jnp.float32), 0.25, 1.75)
    conv_weight = normal_values(seeds[3], (27 * CH, CH), (27 * CH) ** -0.5, 0.0625, ((1, 4),))
    frame_list = draw_frame_list(jax.random.fold_in(seeds[11], 71), 0)
    reward_scale = jnp.clip(jnp.exp(math.log(2.0) - 1.3862944 * jax.random.uniform(seeds[5], (PICKED,), jnp.float32) ** level_of(seeds[5], (PICKED,), ((0, 64),), -0.2, 0.2)), 0.5, 2.0)
    patch_weight = normal_values(seeds[6], (4 * CH, VW), (4 * CH) ** -0.5, 0.15625)
    ln_gain = jnp.clip(1.0 + 0.15 * jax.random.normal(seeds[7], (2, VW), jnp.float32), 0.25, 1.75)
    qkv_weight = normal_values(seeds[8], (VW, 3 * VW), VW ** -0.5, 0.1875, ((1, 4),))
    out_weight = normal_values(seeds[9], (VW, VW), VW ** -0.5, 0.1875, ((0, 4),))
    head_vec = normal_values(seeds[10], (VW,), 0.25, 1.5, (), jnp.float32)
    return dict(latents=latents, conv_in_weight=conv_in_weight, norm_gain=norm_gain, conv_weight=conv_weight, frame_list=frame_list, reward_scale=reward_scale, patch_weight=patch_weight, ln_gain=ln_gain, qkv_weight=qkv_weight, out_weight=out_weight, head_vec=head_vec)


norm_epsilon = 1e-06
layer_epsilon = 1e-05

def gather_columns(padded, frames, height_in, width_in):
    windows = []
    for time_lag in range(3):
        for row_lag in range(3):
            for col_lag in range(3):
                windows.append(padded[time_lag:time_lag + frames, row_lag:row_lag + height_in, col_lag:col_lag + width_in])
    stacked = jnp.concatenate(windows, axis=-1)
    return stacked.reshape(frames * height_in * width_in, stacked.shape[-1])

def scatter_columns(columns, shape, frames, height_in, width_in):
    blank_ext = jnp.zeros(shape, jnp.float32)
    _, pullback = jax.vjp(lambda padded: gather_columns(padded, frames, height_in, width_in), blank_ext)
    return pullback(columns)[0]

def contract_last(left, right):
    return lax.dot_general(left, right, (((1,), (1,)), ((), ())), preferred_element_type=jnp.float32)

def activate(volume, scaling):
    inverse = lax.rsqrt(lax.optimization_barrier(jnp.mean(volume * volume, axis=-1, keepdims=True)) + norm_epsilon)
    return jax.nn.silu(volume * inverse * scaling)

def layer_norm(volume, scaling):
    center = lax.optimization_barrier(jnp.mean(volume, axis=-1, keepdims=True))
    spread = lax.optimization_barrier(jnp.mean((volume - center) ** 2, axis=-1, keepdims=True))
    return (volume - center) * lax.rsqrt(spread + layer_epsilon) * scaling

def layer_norm_back(volume, scaling, cotangent):
    center = lax.optimization_barrier(jnp.mean(volume, axis=-1, keepdims=True))
    spread = lax.optimization_barrier(jnp.mean((volume - center) ** 2, axis=-1, keepdims=True))
    inverse = lax.rsqrt(spread + layer_epsilon)
    whitened = (volume - center) * inverse
    scaled_grad = cotangent * scaling
    return inverse * (scaled_grad - lax.optimization_barrier(jnp.mean(scaled_grad, axis=-1, keepdims=True)) - whitened * lax.optimization_barrier(jnp.mean(scaled_grad * whitened, axis=-1, keepdims=True)))

def patchify(picture):
    height_in, width_in, channels = picture.shape
    blocks = picture.reshape(height_in // 2, 2, width_in // 2, 2, channels).transpose(0, 2, 1, 3, 4)
    return blocks.reshape(height_in // 2 * (width_in // 2), 4 * channels)

def unpatchify(tokens_in, height_in, width_in, channels):
    blocks = tokens_in.reshape(height_in // 2, width_in // 2, 2, 2, channels).transpose(0, 2, 1, 3, 4)
    return blocks.reshape(height_in, width_in, channels)

def convolve(volume, weight):
    clip_set = volume.reshape(CLIPS, CLIP_FR, HEIGHT, COLS, volume.shape[-1])

    def per_clip(clip_frames):
        padded = jnp.pad(clip_frames, ((2, 0), (1, 1), (1, 1), (0, 0)))
        return jnp.dot(gather_columns(padded, CLIP_FR, HEIGHT, COLS), weight, preferred_element_type=jnp.float32)
    result = lax.map(per_clip, clip_set)
    return result.reshape(FRAMES, HEIGHT, COLS, weight.shape[1])

def convolve_back(cotangent, weight, channels):
    clip_set = cotangent.reshape(CLIPS, CLIP_FR * HEIGHT * COLS, cotangent.shape[-1])

    def per_clip(clip_grad):
        columns = contract_last(clip_grad, weight)
        padded = scatter_columns(columns, (CLIP_FR + 2, HEIGHT + 2, COLS + 2, channels), CLIP_FR, HEIGHT, COLS)
        return padded[2:, 1:-1, 1:-1]
    result = lax.map(per_clip, clip_set)
    return result.reshape(FRAMES, HEIGHT, COLS, channels)

def score_frame(picture, weighting, patch_weight, ln_gain, qkv_weight, out_weight, head_vec):
    scale_attn = HD ** (-0.5)
    patches = patchify(picture)
    tokens_x = jnp.dot(patches, patch_weight, preferred_element_type=jnp.float32).astype(jnp.bfloat16)
    normed_in = layer_norm(tokens_x.astype(jnp.float32), ln_gain[0]).astype(jnp.bfloat16)
    qkv = jnp.dot(normed_in, qkv_weight, preferred_element_type=jnp.float32).astype(jnp.bfloat16)
    qkv = qkv.reshape(TOKENS, HEADS, 3, HD).astype(jnp.float32)
    query, key_part, value_part = (qkv[:, :, 0], qkv[:, :, 1], qkv[:, :, 2])
    scores = jnp.einsum('qhd,khd->hqk', query, key_part) * scale_attn
    attention = jax.nn.softmax(scores, axis=-1)
    attn_low = attention.astype(jnp.bfloat16)
    mixed = jnp.einsum('hqk,khd->qhd', attn_low.astype(jnp.float32), value_part).astype(jnp.bfloat16).reshape(TOKENS, VW)
    resid = tokens_x.astype(jnp.float32) + jnp.dot(mixed, out_weight, preferred_element_type=jnp.float32)
    normed_out = layer_norm(resid, ln_gain[1])
    reward = jnp.sum(normed_out * head_vec) / TOKENS
    grad_norm = jnp.broadcast_to(weighting / TOKENS * head_vec, resid.shape)
    grad_resid = layer_norm_back(resid, ln_gain[1], grad_norm)
    grad_mixed = contract_last(grad_resid.astype(jnp.bfloat16), out_weight).astype(jnp.bfloat16)
    grad_mixed = grad_mixed.reshape(TOKENS, HEADS, HD).astype(jnp.float32)
    grad_attn = jnp.einsum('qhd,khd->hqk', grad_mixed, value_part)
    grad_scores = (attention * (grad_attn - lax.optimization_barrier(jnp.sum(grad_attn * attention, axis=-1, keepdims=True))) * scale_attn).astype(jnp.bfloat16).astype(jnp.float32)
    grad_query = jnp.einsum('hqk,khd->qhd', grad_scores, key_part).astype(jnp.bfloat16)
    grad_keyset = jnp.einsum('hqk,qhd->khd', grad_scores, query).astype(jnp.bfloat16)
    grad_values = jnp.einsum('hqk,qhd->khd', attn_low.astype(jnp.float32), grad_mixed).astype(jnp.bfloat16)
    grad_qkv = jnp.stack([grad_query, grad_keyset, grad_values], axis=2).reshape(TOKENS, 3 * VW)
    grad_normed = contract_last(grad_qkv, qkv_weight)
    grad_tokens = (grad_resid + layer_norm_back(tokens_x.astype(jnp.float32), ln_gain[0], grad_normed)).astype(jnp.bfloat16)
    grad_patch = contract_last(grad_tokens, patch_weight).astype(jnp.bfloat16)
    return (reward, unpatchify(grad_patch, HEIGHT, COLS, CH))

def reference(latents, conv_in_weight, norm_gain, conv_weight, frame_list, reward_scale, patch_weight, ln_gain, qkv_weight, out_weight, head_vec):
    volume = latents.reshape(FRAMES, HEIGHT, COLS, LAT)
    first = convolve(volume, conv_in_weight).astype(jnp.bfloat16)
    first_f = first.astype(jnp.float32)
    active = activate(first_f, norm_gain).astype(jnp.bfloat16)
    feats = (first_f + convolve(active, conv_weight)).astype(jnp.bfloat16)
    chosen = feats[frame_list]

    def per_frame(pair):
        return score_frame(pair[0], pair[1], patch_weight, ln_gain, qkv_weight, out_weight, head_vec)
    rewards, frame_grads = lax.map(per_frame, (chosen, reward_scale))
    grad_feats = jnp.zeros(feats.shape, jnp.bfloat16).at[frame_list].add(frame_grads)
    grad_active = convolve_back(grad_feats, conv_weight, CH)
    _, pullback = jax.vjp(lambda volume_in: activate(volume_in, norm_gain), first_f)
    grad_first = (grad_feats.astype(jnp.float32) + pullback(grad_active)[0]).astype(jnp.bfloat16)
    grad_latent = convolve_back(grad_first, conv_in_weight, LAT)
    return (rewards, grad_latent.reshape(FRAMES, HEIGHT, LAT_COLS))
```

```python
import functools

import jax
import jax.numpy as jnp
from jax import lax
from jax.experimental import pallas as pl
from jax.experimental.pallas import tpu as pltpu
from jax.sharding import PartitionSpec as P

LAT = 16
CH = 384
VW = 1024
HD = 64
COLS = 8
ROWS = 32
CLIP_FR = 16
FR_DEV = 2
CLIP_DEV = CLIP_FR // FR_DEV
SP = 4
OUT_CH = CH // SP
LOCAL_HEADS = 4
TOKENS = 64
CELLS = ROWS * COLS
HALF = 64
MESH = pl.DeviceIdType.MESH

norm_epsilon = 1e-06
layer_epsilon = 1e-05

f32 = jnp.float32
bf16 = jnp.bfloat16


def dot(left, right):
    return lax.dot_general(left, right, (((1,), (0,)), ((), ())), preferred_element_type=f32)


def dot_last(left, right):
    return lax.dot_general(left, right, (((1,), (1,)), ((), ())), preferred_element_type=f32)


def dot_first(left, right):
    return lax.dot_general(left, right, (((0,), (0,)), ((), ())), preferred_element_type=f32)


def iota(shape, dim):
    return lax.broadcasted_iota(jnp.int32, shape, dim)


def one_hot(condition):
    return jnp.where(condition, 1.0, 0.0).astype(bf16)


def row_mean(value):
    return jnp.sum(value, axis=-1, keepdims=True) * (1.0 / value.shape[-1])


def layer_stats(volume):
    center = row_mean(volume)
    moved = volume - center
    inverse = lax.rsqrt(row_mean(moved * moved) + layer_epsilon)
    return moved * inverse, inverse


def layer_back(whitened, inverse, scaled_grad):
    return inverse * (
        scaled_grad - row_mean(scaled_grad) - whitened * row_mean(scaled_grad * whitened)
    )


def shifted(value, offset):
    if offset == 0:
        return value
    blank = jnp.zeros(value.shape[:-2] + (1, value.shape[-1]), value.dtype)
    if offset > 0:
        return jnp.concatenate([value[..., 1:, :], blank], axis=-2)
    return jnp.concatenate([blank, value[..., :-1, :]], axis=-2)


def spread(pick, dst, send, recv, count, here, place):
    copies = []
    for step in range(1, count):
        peer = lax.rem(here + step, count)
        copy = pltpu.make_async_remote_copy(
            src_ref=pick(peer),
            dst_ref=dst.at[here],
            send_sem=send.at[step],
            recv_sem=recv.at[step],
            device_id=place(peer),
            device_id_type=MESH,
        )
        copy.start()
        copies.append(copy)
    return copies


def wait_all(copies):
    for copy in copies:
        copy.wait()


def kernel(
    lat_ref,
    list_ref,
    scale_ref,
    gain_ref,
    wi_ref,
    ln_ref,
    head_ref,
    wc_hbm,
    pw_hbm,
    qw_hbm,
    ow_hbm,
    grad_ref,
    reward_ref,
    wc,
    pw,
    qw,
    ow,
    wi_pad,
    lat_seq,
    lat_sp,
    z_ref,
    rolled,
    cols,
    first,
    act,
    feat,
    part,
    rim,
    patch_out,
    patch_in,
    lat_back,
    band_out,
    band_in,
    placed,
    clip_out,
    clip_in,
    back_cols,
    load_sem,
    seq_sems,
    sp_sems,
):
    seq = lax.axis_index("seq")
    sp = lax.axis_index("sp")
    local = lax.rem(seq, CLIP_DEV)
    base = seq - local

    def in_clip(peer):
        return (base + peer, sp)

    def in_band(peer):
        return (seq, peer)

    barrier = pltpu.get_barrier_semaphore()
    for step in range(1, CLIP_DEV):
        pl.semaphore_signal(
            barrier,
            inc=1,
            device_id=in_clip(lax.rem(local + step, CLIP_DEV)),
            device_id_type=MESH,
        )
    for step in range(1, SP):
        pl.semaphore_signal(
            barrier, inc=1, device_id=in_band(lax.rem(sp + step, SP)), device_id_type=MESH
        )
    loads = [
        pltpu.make_async_copy(source, target, load_sem.at[i])
        for i, (source, target) in enumerate(
            ((wc_hbm, wc), (pw_hbm, pw), (qw_hbm, qw), (ow_hbm, ow))
        )
    ]
    for load in loads:
        load.start()

    lat_seq[0:2] = jnp.zeros((2, 16, 128), bf16)
    own = lat_ref[...].reshape(FR_DEV * ROWS, 32)
    packed = jnp.zeros((16, 128), f32)
    for j in range(4):
        spot = one_hot(iota((32, 128), 1) == iota((32, 128), 0) + 32 * j)
        packed = packed + dot(own[16 * j : 16 * j + 16], spot)
    lat_seq[pl.ds(2 + local, 1)] = packed.astype(bf16)[None]

    pl.semaphore_wait(barrier, CLIP_DEV - 1 + SP - 1)

    copies = []
    for step in range(1, CLIP_DEV):
        peer = lax.rem(local + step, CLIP_DEV)
        copy = pltpu.make_async_remote_copy(
            src_ref=lat_seq.at[pl.ds(2 + local, 1)],
            dst_ref=lat_seq.at[pl.ds(2 + local, 1)],
            send_sem=seq_sems.at[0, step],
            recv_sem=seq_sems.at[1, step],
            device_id=in_clip(peer),
            device_id_type=MESH,
        )
        copy.start()
        copies.append(copy)

    wi_pad[...] = jnp.zeros((640, CH), bf16)
    for tap in range(9):
        start = 128 * (tap // 2) + HALF * (tap % 2)
        wi_pad[start : start + 48] = wi_ref[48 * tap : 48 * tap + 48]
    act[...] = jnp.zeros(act.shape, bf16)
    rim[...] = jnp.zeros(rim.shape, bf16)
    lat_back[...] = jnp.zeros(lat_back.shape, f32)
    placed[...] = jnp.zeros(placed.shape, f32)
    row, col = iota((512, 512), 0), iota((512, 512), 1)
    swap = one_hot(
        ((row >> 7) == ((col >> 5) & 3)) & (((row >> 5) & 3) == (col >> 7)) & ((row & 31) == (col & 31))
    )
    row, col = iota((256, 256), 0), iota((256, 256), 1)
    kind, token = row >> 6, row & 63
    to_patch = one_hot(
        col == (2 * (token >> 4) + (kind & 1)) * ROWS + 2 * (token & 15) + (kind >> 1)
    )
    own_channels = one_hot(iota((CH, OUT_CH), 0) == iota((CH, OUT_CH), 1) + sp * OUT_CH)

    wait_all(copies)

    where = lax.rem(list_ref[seq], CLIP_FR)
    chunk, odd = lax.div(where, 2), lax.rem(where, 2)
    lat_sp[pl.ds(sp, 1)] = lat_seq[pl.ds(chunk, 3)].reshape(1, 48, 128)
    copies = spread(
        lambda peer: lat_sp.at[sp], lat_sp, sp_sems.at[0], sp_sems.at[1], SP, sp, in_band
    )
    wait_all(copies)
    wide = jnp.concatenate([lat_sp[s] for s in range(SP)], axis=1)
    spots = dot(wide, swap)
    for c in range(3):
        for j in range(4):
            z_ref[2 * c + j // 2, 16 * (j % 2) : 16 * (j % 2) + 16] = spots[
                16 * c : 16 * c + 16, 128 * j : 128 * j + 128
            ]
    z = z_ref[pl.ds(odd, 5)]
    taps = jnp.stack([shifted(z, dr - 1) for dr in range(3)], axis=1).reshape(480, 128)
    for k in range(8):
        rolled[k] = (taps if k == 0 else pltpu.roll(taps, 16 * k, 1)).reshape(15, ROWS, 128)

    low_lanes = iota((ROWS, 128), 1) < HALF
    lane_col = (iota((ROWS, 128), 1) & (HALF - 1)) >> 4

    def build(c, carry):
        source_col = lane_col + (c - 1)
        inside = (source_col >= 0) & (source_col < COLS)
        even, second = lax.rem(9 - c, 8), lax.rem(13 - c, 8)
        for frame in range(3):
            for pair in range(5):
                tap = 2 * pair
                block = rolled[even, 3 * frame + tap]
                if tap + 1 < 9:
                    block = jnp.where(low_lanes, block, rolled[second, 3 * frame + tap + 1])
                cols[frame, c, :, 128 * pair : 128 * pair + 128] = jnp.where(
                    inside, block, 0.0
                ).astype(bf16)
        return carry

    lax.fori_loop(0, COLS, build, 0)

    gain = gain_ref[...]
    for frame in range(3):
        spots = dot(cols[frame].reshape(CELLS, 640), wi_pad[...])
        first[frame] = spots.astype(bf16).reshape(COLS, ROWS, CH)

    def activate(i, carry):
        frame, c = i // 2, lax.rem(i, 2) * 4
        h = first[frame, pl.ds(c, 4)].astype(f32)
        unit = h * lax.rsqrt(row_mean(h * h) + norm_epsilon) * gain
        value = unit * jax.nn.sigmoid(unit)
        for dr in range(3):
            act[dr, frame, pl.ds(c + 1, 4)] = shifted(value, dr - 1).astype(bf16)
        return carry

    lax.fori_loop(0, 6, activate, 0)

    loads[0].wait()
    total = dot(first[2].reshape(CELLS, CH), own_channels)
    for dt in range(3):
        for dr in range(3):
            window = jnp.concatenate(
                [act[dr, dt, dc : dc + COLS].reshape(CELLS, CH) for dc in range(3)], axis=1
            )
            start = (3 * dt + dr) * 3 * CH
            total = total + dot_last(window, wc[:, start : start + 3 * CH])
    feat[pl.ds(sp, 1)] = dot(to_patch, total.astype(bf16)).astype(bf16)[None]

    copies = spread(
        lambda peer: feat.at[sp], feat, sp_sems.at[2], sp_sems.at[3], SP, sp, in_band
    )
    loads[1].wait()
    loads[2].wait()
    loads[3].wait()
    wait_all(copies)

    patches = jnp.concatenate(
        [feat[s, TOKENS * k : TOKENS * k + TOKENS] for k in range(4) for s in range(SP)], axis=1
    )
    x = dot(patches, pw[...]).astype(bf16).astype(f32)
    white_in, inverse_in = layer_stats(x)
    gain_in, gain_out = ln_ref[0:1], ln_ref[1:2]
    qkv = dot((white_in * gain_in).astype(bf16), qw[...]).astype(bf16)
    heads = []
    mixed = []
    for head in range(LOCAL_HEADS):
        start = 3 * HD * head
        q, k, v = (qkv[:, start + HD * i : start + HD * i + HD] for i in range(3))
        scores = dot_last(q, k) * (HD**-0.5)
        weights = jnp.exp(scores - jnp.max(scores, axis=-1, keepdims=True))
        probs = weights / jnp.sum(weights, axis=-1, keepdims=True)
        probs_low = probs.astype(bf16)
        mixed.append(dot(probs_low, v).astype(bf16))
        heads.append((q, k, v, probs, probs_low))
    part[pl.ds(sp, 1)] = dot(jnp.concatenate(mixed, axis=1), ow[...]).astype(bf16)[None]
    copies = spread(
        lambda peer: part.at[sp], part, sp_sems.at[4], sp_sems.at[5], SP, sp, in_band
    )
    wait_all(copies)
    y = x
    for s in range(SP):
        y = y + part[s].astype(f32)
    white_out, inverse_out = layer_stats(y)
    vector = head_ref[...]
    reward = jnp.sum(white_out * gain_out * vector, axis=1, keepdims=True)
    reward_ref[...] = jnp.sum(reward, axis=0, keepdims=True) * (1.0 / TOKENS)
    scaled = (scale_ref[0] * (1.0 / TOKENS)) * vector * gain_out
    dy = layer_back(white_out, inverse_out, jnp.broadcast_to(scaled, y.shape))
    do = dot_last(dy.astype(bf16), ow[...]).astype(bf16)
    grads = []
    for head in range(LOCAL_HEADS):
        q, k, v, probs, probs_low = heads[head]
        d_out = do[:, HD * head : HD * head + HD]
        d_probs = dot_last(d_out, v)
        d_scores = (
            probs
            * (d_probs - jnp.sum(d_probs * probs, axis=-1, keepdims=True))
            * (HD**-0.5)
        ).astype(bf16)
        grads.append(dot(d_scores, k).astype(bf16))
        grads.append(dot_first(d_scores, q).astype(bf16))
        grads.append(dot_first(probs_low, d_out).astype(bf16))
    da = dot_last(jnp.concatenate(grads, axis=1), qw[...])
    dx = layer_back(white_in, inverse_in, da * gain_in) + dy * (1.0 / SP)
    d_patch = dot_last(dx.astype(bf16), pw[...]).astype(bf16)
    for s in range(SP):
        for k in range(4):
            start = CH * k + OUT_CH * s
            patch_out[s, TOKENS * k : TOKENS * k + TOKENS] = d_patch[:, start : start + OUT_CH]
    copies = spread(
        lambda peer: patch_out.at[peer], patch_in, sp_sems.at[6], sp_sems.at[7], SP, sp, in_band
    )
    patch_in[pl.ds(sp, 1)] = patch_out[pl.ds(sp, 1)]
    wait_all(copies)
    summed = patch_in[0].astype(f32)
    for s in range(1, SP):
        summed = summed + patch_in[s].astype(f32)
    d_feat = dot_first(to_patch, summed.astype(bf16))
    d_cells = d_feat.reshape(COLS, ROWS, OUT_CH)
    for dr in range(3):
        rim[dr, 1 : 1 + COLS] = shifted(d_cells, 1 - dr).astype(bf16)
    d_own = dot_last(d_feat.astype(bf16), own_channels)

    for frame in range(3):
        d_act = jnp.zeros((CELLS, CH), f32)
        for dr in range(3):
            for dc in range(3):
                start = ((3 * frame + dr) * 3 + dc) * CH
                d_act = d_act + dot(
                    rim[dr, 2 - dc : 2 - dc + COLS].reshape(CELLS, OUT_CH), wc[:, start : start + CH]
                )
        h = first[frame].reshape(CELLS, CH).astype(f32)
        inverse = lax.rsqrt(row_mean(h * h) + norm_epsilon)
        unit = h * inverse * gain
        gate = jax.nn.sigmoid(unit)
        d_unit = d_act * (gate * (1.0 + unit * (1.0 - gate))) * gain
        d_first = inverse * d_unit - h * (inverse * inverse * inverse * row_mean(d_unit * h))
        if frame == 2:
            d_first = d_first + d_own
        back_cols[frame] = dot_last(d_first.astype(bf16), wi_pad[...]).reshape(COLS, ROWS, 640)

    def collect(c, carry):
        source_col = lane_col + (c - 1)
        inside = (source_col >= 0) & (source_col < COLS)
        low = [jnp.zeros((ROWS, 128), f32)] * 15
        high = [jnp.zeros((ROWS, 128), f32)] * 15
        for frame in range(3):
            for pair in range(5):
                tap = 2 * pair
                block = jnp.where(inside, back_cols[frame, c, :, 128 * pair : 128 * pair + 128], 0.0)
                low[3 * frame + tap] = low[3 * frame + tap] + jnp.where(low_lanes, block, 0.0)
                if tap + 1 < 9:
                    high[3 * frame + tap + 1] = high[3 * frame + tap + 1] + jnp.where(
                        low_lanes, 0.0, block
                    )
        joined = jnp.concatenate(low, axis=0) + pltpu.roll(jnp.concatenate(high, axis=0), HALF, 1)
        return carry + pltpu.roll(joined, lax.rem(16 * c + 112, 128), 1)

    gathered = lax.fori_loop(0, COLS, collect, jnp.zeros((480, 128), f32))
    gathered = gathered.reshape(5, 3, ROWS, 128)
    lat_back[1:6] = (
        gathered[:, 1] + shifted(gathered[:, 0], 1) + shifted(gathered[:, 2], -1)
    )
    aligned = lat_back[pl.ds(1 - odd, 6)].astype(bf16)
    wide = jnp.concatenate(
        [
            jnp.concatenate(
                [aligned[2 * c + j // 2, 16 * (j % 2) : 16 * (j % 2) + 16] for j in range(4)], axis=1
            )
            for c in range(3)
        ],
        axis=0,
    )
    bands = dot(wide, swap).astype(bf16)
    for s in range(SP):
        band_out[s] = bands[:, 128 * s : 128 * s + 128]
    copies = spread(
        lambda peer: band_out.at[peer], band_in, sp_sems.at[8], sp_sems.at[9], SP, sp, in_band
    )
    band_in[pl.ds(sp, 1)] = band_out[pl.ds(sp, 1)]
    wait_all(copies)
    summed = band_in[0].astype(f32)
    for s in range(1, SP):
        summed = summed + band_in[s].astype(f32)
    placed[5:8] = summed.reshape(3, 16, 128)
    clip_out[...] = placed[pl.ds(7 - chunk, 8)].astype(bf16)
    copies = spread(
        lambda peer: clip_out.at[peer],
        clip_in,
        seq_sems.at[2],
        seq_sems.at[3],
        CLIP_DEV,
        local,
        in_clip,
    )
    clip_in[pl.ds(local, 1)] = clip_out[pl.ds(local, 1)]
    wait_all(copies)
    summed = clip_in[0].astype(f32)
    for s in range(1, CLIP_DEV):
        summed = summed + clip_in[s].astype(f32)
    grad_ref[...] = summed


def body(
    latents,
    conv_in_weight,
    norm_gain,
    conv_weight,
    frame_list,
    reward_scale,
    patch_weight,
    ln_gain,
    qkv_weight,
    out_weight,
    head_vec,
):
    vmem = pl.BlockSpec(memory_space=pltpu.VMEM)
    smem = pl.BlockSpec(memory_space=pltpu.SMEM)
    anywhere = pl.BlockSpec(memory_space=pl.ANY)
    grad, reward = pl.pallas_call(
        kernel,
        out_shape=(
            jax.ShapeDtypeStruct((16, 128), f32),
            jax.ShapeDtypeStruct((1, 1), f32),
        ),
        in_specs=[vmem, smem, smem, vmem, vmem, vmem, vmem] + [anywhere] * 4,
        out_specs=(vmem, vmem),
        scratch_shapes=[
            pltpu.VMEM((OUT_CH, 27 * CH), bf16),
            pltpu.VMEM((4 * CH, VW), bf16),
            pltpu.VMEM((VW, 3 * HD * LOCAL_HEADS), bf16),
            pltpu.VMEM((HD * LOCAL_HEADS, VW), bf16),
            pltpu.VMEM((640, CH), bf16),
            pltpu.VMEM((2 + CLIP_DEV, 16, 128), bf16),
            pltpu.VMEM((SP, 48, 128), bf16),
            pltpu.VMEM((6, ROWS, 128), f32),
            pltpu.VMEM((8, 15, ROWS, 128), f32),
            pltpu.VMEM((3, COLS, ROWS, 640), bf16),
            pltpu.VMEM((3, COLS, ROWS, CH), bf16),
            pltpu.VMEM((3, 3, COLS + 2, ROWS, CH), bf16),
            pltpu.VMEM((SP, CELLS, OUT_CH), bf16),
            pltpu.VMEM((SP, TOKENS, VW), bf16),
            pltpu.VMEM((3, COLS + 2, ROWS, OUT_CH), bf16),
            pltpu.VMEM((SP, CELLS, OUT_CH), bf16),
            pltpu.VMEM((SP, CELLS, OUT_CH), bf16),
            pltpu.VMEM((7, ROWS, 128), f32),
            pltpu.VMEM((SP, 48, 128), bf16),
            pltpu.VMEM((SP, 48, 128), bf16),
            pltpu.VMEM((15, 16, 128), f32),
            pltpu.VMEM((CLIP_DEV, 16, 128), bf16),
            pltpu.VMEM((CLIP_DEV, 16, 128), bf16),
            pltpu.VMEM((3, COLS, ROWS, 640), f32),
            pltpu.SemaphoreType.DMA((4,)),
            pltpu.SemaphoreType.DMA((4, CLIP_DEV)),
            pltpu.SemaphoreType.DMA((10, SP)),
        ],
        compiler_params=pltpu.CompilerParams(
            collective_id=0, has_side_effects=True, vmem_limit_bytes=48 * 1024 * 1024
        ),
        name="reward_step",
    )(
        latents,
        frame_list,
        reward_scale,
        norm_gain.reshape(1, CH),
        conv_in_weight,
        ln_gain,
        head_vec.reshape(1, VW),
        conv_weight.T,
        patch_weight,
        qkv_weight,
        out_weight,
    )
    spread_rows = grad.reshape(16, 4, 32).transpose(1, 0, 2)
    return (reward.reshape(1), spread_rows.reshape(FR_DEV, ROWS, 32))


def solution(mesh):
    in_specs = (
        P("seq", None, "sp"),
        P(),
        P(),
        P(None, "sp"),
        P(),
        P("seq"),
        P(),
        P(),
        P(None, "sp"),
        P("sp", None),
        P(),
    )
    out_specs = (P("seq"), P("seq", None, "sp"))
    return jax.shard_map(body, mesh=mesh, in_specs=in_specs, out_specs=out_specs, check_vma=False)
```

```python
import functools

import jax
import jax.numpy as jnp
from jax import lax
from jax.experimental import pallas as pl
from jax.experimental.pallas import tpu as pltpu
from jax.sharding import PartitionSpec as P

LAT = 16
CH = 384
VW = 1024
HD = 64
COLS = 8
ROWS = 32
CLIP_FR = 16
FR_DEV = 2
CLIP_DEV = CLIP_FR // FR_DEV
SP = 4
OUT_CH = CH // SP
LOCAL_HEADS = 4
TOKENS = 64
CELLS = ROWS * COLS
HALF = 64
MESH = pl.DeviceIdType.MESH

norm_epsilon = 1e-06
layer_epsilon = 1e-05

f32 = jnp.float32
bf16 = jnp.bfloat16


def dot(left, right):
    return lax.dot_general(left, right, (((1,), (0,)), ((), ())), preferred_element_type=f32)


def dot_last(left, right):
    return lax.dot_general(left, right, (((1,), (1,)), ((), ())), preferred_element_type=f32)


def dot_first(left, right):
    return lax.dot_general(left, right, (((0,), (0,)), ((), ())), preferred_element_type=f32)


def iota(shape, dim):
    return lax.broadcasted_iota(jnp.int32, shape, dim)


def one_hot(condition):
    return jnp.where(condition, 1.0, 0.0).astype(bf16)


def row_mean(value):
    return jnp.sum(value, axis=-1, keepdims=True) * (1.0 / value.shape[-1])


def layer_stats(volume):
    center = row_mean(volume)
    moved = volume - center
    inverse = lax.rsqrt(row_mean(moved * moved) + layer_epsilon)
    return moved * inverse, inverse


def layer_back(whitened, inverse, scaled_grad):
    return inverse * (
        scaled_grad - row_mean(scaled_grad) - whitened * row_mean(scaled_grad * whitened)
    )


def shifted(value, offset):
    if offset == 0:
        return value
    blank = jnp.zeros(value.shape[:-2] + (1, value.shape[-1]), value.dtype)
    if offset > 0:
        return jnp.concatenate([value[..., 1:, :], blank], axis=-2)
    return jnp.concatenate([blank, value[..., :-1, :]], axis=-2)


def moved(value, offset):
    if offset == 0:
        return value
    blank = jnp.zeros((1,) + value.shape[1:], value.dtype)
    if offset > 0:
        return jnp.concatenate([value[1:], blank], axis=0)
    return jnp.concatenate([blank, value[:-1]], axis=0)


def start_copy(source, target, send, recv, device, pending):
    copy = pltpu.make_async_remote_copy(
        src_ref=source,
        dst_ref=target,
        send_sem=send,
        recv_sem=recv,
        device_id=device,
        device_id_type=MESH,
    )
    copy.start()
    pending.append(copy)
    return copy


def exchange(pick, slots, sems, here, place, count, pending):
    copies = {}
    for step in range(1, count):
        peer = lax.rem(here + step, count)
        copies[step] = start_copy(
            pick(step), slots.at[step], sems.at[0, step], sems.at[1, step], place(peer), pending
        )
    return copies


def wait_all(copies):
    for copy in copies.values():
        copy.wait_recv()


def kernel(
    lat_hbm,
    list_hbm,
    scale_hbm,
    gain_hbm,
    wi_hbm,
    ln_hbm,
    head_hbm,
    conv_hbm,
    patch_hbm,
    qkv_hbm,
    out_hbm,
    grad_ref,
    reward_ref,
    lat_ref,
    list_ref,
    scale_ref,
    gain_ref,
    ln_ref,
    head_ref,
    conv_ref,
    patch_ref,
    qkv_ref,
    out_ref,
    wi_pad,
    lat_seq,
    lat_sp,
    z_ref,
    rolled,
    cols,
    first,
    slope,
    act,
    feat,
    embed,
    mix,
    patch_out,
    patch_in,
    lat_back,
    band_out,
    band_in,
    placed,
    clip_out,
    clip_in,
    back_cols,
    load_sem,
    conv_sem,
    patch_sem,
    seq_sems,
    clip_sems,
    lat_sems,
    feat_sems,
    mix_sems,
    patch_sems,
    band_sems,
    half_sems,
    pair_sems,
):
    seq = lax.axis_index("seq")
    sp = lax.axis_index("sp")
    local = lax.rem(seq, CLIP_DEV)
    base = seq - local

    def in_clip(peer):
        return (base + peer, sp)

    def in_band(peer):
        return (seq, peer)

    loads = {}
    pending = []

    def load(name, source, target, sem):
        copy = pltpu.make_async_copy(source, target, sem)
        copy.start()
        loads.setdefault(name, []).append(copy)

    def loaded(*names):
        for name in names:
            for copy in loads.pop(name):
                copy.wait()

    for i, (name, source, target) in enumerate(
        (
            ("lat", lat_hbm, lat_ref),
            ("list", list_hbm, list_ref),
            ("gain", gain_hbm, gain_ref),
            ("wi", wi_hbm, wi_pad.at[0 : 27 * LAT]),
            ("ln", ln_hbm, ln_ref),
            ("head", head_hbm, head_ref),
            ("scale", scale_hbm, scale_ref),
        )
    ):
        load(name, source, target, load_sem.at[i])

    barrier = pltpu.get_barrier_semaphore()
    for step in range(1, CLIP_DEV):
        pl.semaphore_signal(
            barrier,
            inc=1,
            device_id=in_clip(lax.rem(local + step, CLIP_DEV)),
            device_id_type=MESH,
        )
    for step in range(1, SP):
        pl.semaphore_signal(
            barrier, inc=1, device_id=in_band(lax.rem(sp + step, SP)), device_id_type=MESH
        )

    lat_seq[0:2] = jnp.zeros((2, 16, 128), bf16)
    loaded("lat")
    own = lat_ref[...].reshape(FR_DEV * ROWS, 32)
    packed = jnp.zeros((16, 128), f32)
    for j in range(4):
        spot = one_hot(iota((32, 128), 1) == iota((32, 128), 0) + 32 * j)
        packed = packed + dot(own[16 * j : 16 * j + 16], spot)
    lat_seq[pl.ds(2 + local, 1)] = packed.astype(bf16)[None]

    pl.semaphore_wait(barrier, CLIP_DEV - 1 + SP - 1)

    mine = lat_seq.at[pl.ds(2 + local, 1)]
    copies = {}
    for step in range(1, CLIP_DEV):
        copies[step] = start_copy(
            mine,
            mine,
            seq_sems.at[0, step],
            seq_sems.at[1, step],
            in_clip(lax.rem(local + step, CLIP_DEV)),
            pending,
        )

    half = lax.rem(local, 2)
    out_copies = {}
    for step in range(1, SP):
        out_copies[step] = start_copy(
            out_hbm.at[pl.ds(pl.multiple_of(half * 128, 128), 128)],
            out_ref.at[pl.ds(pl.multiple_of(sp * 256 + half * 128, 128), 128)],
            half_sems.at[0, step],
            half_sems.at[1, step],
            in_band(lax.rem(sp + step, SP)),
            pending,
        )

    for dt in range(3):
        for near in range(9):
            load(
                "conv",
                conv_hbm.at[:, CH * (9 * dt + near) : CH * (9 * dt + near + 1)],
                conv_ref.at[OUT_CH * near : OUT_CH * near + OUT_CH, CH * dt : CH * dt + CH],
                conv_sem.at[dt, near],
            )
    for k in range(4):
        for s in range(SP):
            load(
                "patch",
                patch_hbm.at[CH * k + OUT_CH * s : CH * k + OUT_CH * s + OUT_CH],
                patch_ref.at[CH * s + OUT_CH * k : CH * s + OUT_CH * k + OUT_CH],
                patch_sem.at[k, s],
            )
    load("qkv", qkv_hbm, qkv_ref, load_sem.at[7])
    load("out", out_hbm, out_ref.at[pl.ds(pl.multiple_of(sp * 256, 256), 256)], load_sem.at[8])

    wi_pad[27 * LAT :] = jnp.zeros((512 - 27 * LAT, CH), bf16)
    lat_back[...] = jnp.zeros(lat_back.shape, f32)
    placed[...] = jnp.zeros(placed.shape, f32)
    row, col = iota((512, 512), 0), iota((512, 512), 1)
    swap = one_hot(
        ((row >> 7) == ((col >> 5) & 3)) & (((row >> 5) & 3) == (col >> 7)) & ((row & 31) == (col & 31))
    )
    row, col = iota((256, 256), 0), iota((256, 256), 1)
    kind, token = row >> 6, row & 63
    to_patch = one_hot(
        col == (2 * (token >> 4) + (kind & 1)) * ROWS + 2 * (token & 15) + (kind >> 1)
    )
    own_channels = one_hot(iota((CH, OUT_CH), 0) == iota((CH, OUT_CH), 1) + sp * OUT_CH)

    wait_all(copies)

    loaded("list")
    where = lax.rem(list_ref[seq], CLIP_FR)
    chunk, odd = lax.div(where, 2), lax.rem(where, 2)
    lat_sp[pl.ds(sp, 1)] = lat_seq[pl.ds(chunk, 3)].reshape(1, 48, 128)
    copies = {}
    for step in range(1, SP):
        copies[step] = start_copy(
            lat_sp.at[sp],
            lat_sp.at[sp],
            lat_sems.at[0, step],
            lat_sems.at[1, step],
            in_band(lax.rem(sp + step, SP)),
            pending,
        )
    wait_all(copies)
    wide = jnp.concatenate([lat_sp[s] for s in range(SP)], axis=1)
    spots = dot(wide, swap)
    for c in range(3):
        for j in range(4):
            z_ref[2 * c + j // 2, 16 * (j % 2) : 16 * (j % 2) + 16] = spots[
                16 * c : 16 * c + 16, 128 * j : 128 * j + 128
            ]
    z = z_ref[pl.ds(odd, 5)]
    taps = jnp.stack([shifted(z, dr - 1) for dr in range(3)], axis=1).reshape(480, 128)
    for k in range(8):
        rolled[k] = (taps if k == 0 else pltpu.roll(taps, 16 * k, 1)).reshape(15, ROWS, 128)

    lane = iota((ROWS, 128), 1)
    pieces = []
    for block in range(4):
        inner = lax.rem(lane + 128 * block, 48) >> 4
        taps_here = [t for t in range(9) if 48 * t < 128 * block + 128 and 48 * t + 48 > 128 * block]
        pieces.append((inner, taps_here))

    def inside(inner, c):
        return ((inner > 0) | (c > 0)) & ((inner < 2) | (c < COLS - 1))

    def build(c, carry):
        for frame in range(3):
            for block, (inner, taps_here) in enumerate(pieces):
                value = None
                for tap in taps_here:
                    part = rolled[lax.rem(3 * tap + 9 - c, 8), 3 * frame + tap]
                    begin = 48 * tap - 128 * block
                    value = part if value is None else jnp.where(lane >= begin, part, value)
                cols[frame, c, :, 128 * block : 128 * block + 128] = jnp.where(
                    inside(inner, c), value, 0.0
                ).astype(bf16)
        return carry

    lax.fori_loop(0, COLS, build, 0, unroll=True)

    loaded("gain", "wi")
    gain = gain_ref[...].reshape(1, CH)
    for frame in range(3):
        spots = dot(cols[frame].reshape(CELLS, 512), wi_pad[...])
        first[frame] = spots.astype(bf16)

    for frame in range(3):
        for half_frame in range(2):
            rows = slice(128 * half_frame, 128 * half_frame + 128)
            h = first[frame, rows].astype(f32)
            unit = h * lax.rsqrt(row_mean(h * h) + norm_epsilon) * gain
            act[rows, CH * frame : CH * frame + CH] = (unit * jax.nn.sigmoid(unit)).astype(bf16)

    loaded("conv")
    spots = dot_last(act[...], conv_ref[...])
    total = dot(first[2], own_channels).reshape(COLS, ROWS, OUT_CH)
    for dr in range(3):
        line = None
        for dc in range(3):
            start = OUT_CH * (3 * dr + dc)
            term = moved(spots[:, start : start + OUT_CH].reshape(COLS, ROWS, OUT_CH), dc - 1)
            line = term if line is None else line + term
        total = total + shifted(line, dr - 1)
    patches = dot(to_patch, total.reshape(CELLS, OUT_CH).astype(bf16))
    feat[0] = jnp.concatenate(
        [patches[TOKENS * k : TOKENS * k + TOKENS] for k in range(4)], axis=1
    ).astype(bf16)

    copies = exchange(
        lambda step: feat.at[0], feat, feat_sems, sp, in_band, SP, pending
    )
    loaded("patch")

    def embed_from(step):
        source = lax.rem(sp + SP - step, SP)
        rows = pl.ds(pl.multiple_of(source * CH, 128), CH)
        embed[pl.ds(source, 1)] = dot(feat[step], patch_ref[rows, :])[None]

    embed_from(0)
    for frame in range(3):
        h = first[frame].astype(f32)
        inverse = lax.rsqrt(row_mean(h * h) + norm_epsilon)
        unit = h * inverse * gain
        gate = jax.nn.sigmoid(unit)
        slope[frame] = gate * (1.0 + unit * (1.0 - gate)) * (gain * inverse)
    pair_copies = {}
    for step in range(1, SP):
        out_copies[step].wait_recv()
        source = lax.rem(sp + SP - step, SP)
        got = out_ref.at[pl.ds(pl.multiple_of(source * 256 + half * 128, 128), 128)]
        pair_copies[step] = start_copy(
            got,
            got,
            pair_sems.at[0, step],
            pair_sems.at[1, step],
            (seq + 1 - 2 * half, sp),
            pending,
        )
    for step in (1, 3, 2):
        copies[step].wait_recv()
        embed_from(step)
    loaded("ln", "qkv", "out", "head", "scale")

    x = embed[0]
    for s in range(1, SP):
        x = x + embed[s]
    x = x.astype(bf16).astype(f32)
    white_in, inverse_in = layer_stats(x)
    gain_in, gain_out = ln_ref[0:1], ln_ref[1:2]
    qkv = dot((white_in * gain_in).astype(bf16), qkv_ref[...]).astype(bf16)
    heads = []
    mixed = []
    for head in range(LOCAL_HEADS):
        start = 3 * HD * head
        q, k, v = (qkv[:, start + HD * i : start + HD * i + HD] for i in range(3))
        scores = dot_last(q, k) * (HD**-0.5)
        weights = jnp.exp(scores - jnp.max(scores, axis=-1, keepdims=True))
        probs = weights / jnp.sum(weights, axis=-1, keepdims=True)
        probs_low = probs.astype(bf16)
        mixed.append(dot(probs_low, v).astype(bf16))
        heads.append((q, k, v, probs, probs_low))
    mix[0] = jnp.concatenate(mixed, axis=1)

    copies = exchange(lambda step: mix.at[0], mix, mix_sems, sp, in_band, SP, pending)

    def project_from(step):
        source = lax.rem(sp + SP - step, SP)
        rows = pl.ds(pl.multiple_of(source * 256, 256), 256)
        embed[pl.ds(source, 1)] = dot(mix[step], out_ref[rows, :])[None]

    project_from(0)
    wait_all(pair_copies)
    for step in (1, 3, 2):
        copies[step].wait_recv()
        project_from(step)

    attended = embed[0]
    for s in range(1, SP):
        attended = attended + embed[s]
    y = x + attended
    white_out, inverse_out = layer_stats(y)
    vector = head_ref[...].reshape(1, VW)
    reward = jnp.sum(white_out * gain_out * vector, axis=1, keepdims=True)
    reward_ref[...] = jnp.sum(reward, axis=0, keepdims=True) * (1.0 / TOKENS)
    scaled = (scale_ref[0] * (1.0 / TOKENS)) * vector * gain_out
    dy = layer_back(white_out, inverse_out, jnp.broadcast_to(scaled, y.shape))
    own_out = out_ref[pl.ds(pl.multiple_of(sp * 256, 256), 256), :]
    do = dot_last(dy.astype(bf16), own_out).astype(bf16)
    grads = []
    for head in range(LOCAL_HEADS):
        q, k, v, probs, probs_low = heads[head]
        d_out = do[:, HD * head : HD * head + HD]
        d_probs = dot_last(d_out, v)
        d_scores = (
            probs
            * (d_probs - jnp.sum(d_probs * probs, axis=-1, keepdims=True))
            * (HD**-0.5)
        ).astype(bf16)
        grads.append(dot(d_scores, k).astype(bf16))
        grads.append(dot_first(d_scores, q).astype(bf16))
        grads.append(dot_first(probs_low, d_out).astype(bf16))
    da = dot_last(jnp.concatenate(grads, axis=1), qkv_ref[...])
    dx = layer_back(white_in, inverse_in, da * gain_in) + dy * (1.0 / SP)
    dx_low = dx.astype(bf16)
    copies = {}
    for step in (2, 1, 3, 0):
        peer = lax.rem(sp + step, SP)
        rows = pl.ds(pl.multiple_of(peer * CH, 128), CH)
        block = dot_last(dx_low, patch_ref[rows, :]).astype(bf16)
        if step == 0:
            patch_in[0] = block
        else:
            patch_out[step] = block
            copies[step] = start_copy(
                patch_out.at[step],
                patch_in.at[step],
                patch_sems.at[0, step],
                patch_sems.at[1, step],
                in_band(peer),
                pending,
            )

    wait_all(copies)

    summed = patch_in[0].astype(f32)
    for s in range(1, SP):
        summed = summed + patch_in[s].astype(f32)
    summed = jnp.concatenate(
        [summed[:, OUT_CH * k : OUT_CH * k + OUT_CH] for k in range(4)], axis=0
    )
    d_feat = dot_first(to_patch, summed.astype(bf16))
    d_cells = d_feat.reshape(COLS, ROWS, OUT_CH)
    lines = [shifted(d_cells, 1 - dr).astype(bf16) for dr in range(3)]
    spread_out = jnp.concatenate(
        [
            moved(lines[dr], 1 - dc).reshape(CELLS, OUT_CH)
            for dr in range(3)
            for dc in range(3)
        ],
        axis=1,
    )
    d_own = dot_last(d_feat.astype(bf16), own_channels)

    for frame in (2, 1, 0):
        d_act = dot(spread_out, conv_ref[:, CH * frame : CH * frame + CH])
        h = first[frame].astype(f32)
        square = row_mean(h * h) + norm_epsilon
        d_unit = d_act * slope[frame]
        d_first = d_unit - h * (row_mean(d_unit * h) / square)
        if frame == 2:
            d_first = d_first + d_own
        back_cols[frame] = dot_last(d_first.astype(bf16), wi_pad[...]).reshape(COLS, ROWS, 512)

    def collect(c, carry):
        totals = list(carry)
        for frame in range(3):
            for block, (inner, taps_here) in enumerate(pieces):
                value = jnp.where(
                    inside(inner, c), back_cols[frame, c, :, 128 * block : 128 * block + 128], 0.0
                )
                for tap in taps_here:
                    begin = 48 * tap - 128 * block
                    within = value
                    if begin > 0:
                        within = jnp.where(lane >= begin, within, 0.0)
                    if begin + 48 < 128:
                        within = jnp.where(lane < begin + 48, within, 0.0)
                    turn = lax.rem(16 * (c + 23 - 3 * tap + 8), 128)
                    totals[3 * frame + tap] = totals[3 * frame + tap] + pltpu.roll(within, turn, 1)
        return tuple(totals)

    gathered = lax.fori_loop(
        0, COLS, collect, tuple(jnp.zeros((ROWS, 128), f32) for _ in range(15)), unroll=True
    )
    gathered = jnp.stack(gathered, axis=0)
    gathered = gathered.reshape(5, 3, ROWS, 128)
    lat_back[1:6] = (
        gathered[:, 1] + shifted(gathered[:, 0], 1) + shifted(gathered[:, 2], -1)
    )
    aligned = lat_back[pl.ds(1 - odd, 6)].astype(bf16)
    wide = jnp.concatenate(
        [
            jnp.concatenate(
                [aligned[2 * c + j // 2, 16 * (j % 2) : 16 * (j % 2) + 16] for j in range(4)], axis=1
            )
            for c in range(3)
        ],
        axis=0,
    )
    bands = dot(wide, swap).astype(bf16)
    for s in range(SP):
        band_out[s] = bands[:, 128 * s : 128 * s + 128]

    copies = exchange(
        lambda step: band_out.at[lax.rem(sp + step, SP)],
        band_in,
        band_sems,
        sp,
        in_band,
        SP,
        pending,
    )
    band_in[pl.ds(0, 1)] = band_out[pl.ds(sp, 1)]
    wait_all(copies)

    summed = band_in[0].astype(f32)
    for s in range(1, SP):
        summed = summed + band_in[s].astype(f32)
    placed[5:8] = summed.reshape(3, 16, 128)
    clip_out[...] = placed[pl.ds(7 - chunk, 8)].astype(bf16)
    copies = exchange(
        lambda step: clip_out.at[lax.rem(local + step, CLIP_DEV)],
        clip_in,
        clip_sems,
        local,
        in_clip,
        CLIP_DEV,
        pending,
    )
    clip_in[pl.ds(0, 1)] = clip_out[pl.ds(local, 1)]
    wait_all(copies)

    summed = clip_in[0].astype(f32)
    for s in range(1, CLIP_DEV):
        summed = summed + clip_in[s].astype(f32)
    grad_ref[...] = summed
    for copy in pending:
        copy.wait_send()


def body(
    latents,
    conv_in_weight,
    norm_gain,
    conv_weight,
    frame_list,
    reward_scale,
    patch_weight,
    ln_gain,
    qkv_weight,
    out_weight,
    head_vec,
):
    vmem = pl.BlockSpec(memory_space=pltpu.VMEM)
    hbm = pl.BlockSpec(memory_space=pltpu.HBM)
    grad, reward = pl.pallas_call(
        kernel,
        out_shape=(
            jax.ShapeDtypeStruct((16, 128), f32),
            jax.ShapeDtypeStruct((1, 1), f32),
        ),
        in_specs=[hbm] * 11,
        out_specs=(vmem, vmem),
        scratch_shapes=[
            pltpu.VMEM((FR_DEV, ROWS, 32), bf16),
            pltpu.SMEM((64,), jnp.int32),
            pltpu.SMEM((1,), f32),
            pltpu.VMEM((CH,), f32),
            pltpu.VMEM((2, VW), f32),
            pltpu.VMEM((VW,), f32),
            pltpu.VMEM((9 * OUT_CH, 3 * CH), bf16),
            pltpu.VMEM((4 * CH, VW), bf16),
            pltpu.VMEM((VW, 3 * HD * LOCAL_HEADS), bf16),
            pltpu.VMEM((VW, VW), bf16),
            pltpu.VMEM((512, CH), bf16),
            pltpu.VMEM((2 + CLIP_DEV, 16, 128), bf16),
            pltpu.VMEM((SP, 48, 128), bf16),
            pltpu.VMEM((6, ROWS, 128), f32),
            pltpu.VMEM((8, 15, ROWS, 128), f32),
            pltpu.VMEM((3, COLS, ROWS, 512), bf16),
            pltpu.VMEM((3, CELLS, CH), bf16),
            pltpu.VMEM((3, CELLS, CH), f32),
            pltpu.VMEM((CELLS, 3 * CH), bf16),
            pltpu.VMEM((SP, TOKENS, CH), bf16),
            pltpu.VMEM((SP, TOKENS, VW), f32),
            pltpu.VMEM((SP, TOKENS, HD * LOCAL_HEADS), bf16),
            pltpu.VMEM((SP, TOKENS, CH), bf16),
            pltpu.VMEM((SP, TOKENS, CH), bf16),
            pltpu.VMEM((7, ROWS, 128), f32),
            pltpu.VMEM((SP, 48, 128), bf16),
            pltpu.VMEM((SP, 48, 128), bf16),
            pltpu.VMEM((15, 16, 128), f32),
            pltpu.VMEM((CLIP_DEV, 16, 128), bf16),
            pltpu.VMEM((CLIP_DEV, 16, 128), bf16),
            pltpu.VMEM((3, COLS, ROWS, 512), f32),
            pltpu.SemaphoreType.DMA((9,)),
            pltpu.SemaphoreType.DMA((3, 9)),
            pltpu.SemaphoreType.DMA((4, SP)),
            pltpu.SemaphoreType.DMA((2, CLIP_DEV)),
            pltpu.SemaphoreType.DMA((2, CLIP_DEV)),
        ]
        + [pltpu.SemaphoreType.DMA((2, SP))] * 7,
        compiler_params=pltpu.CompilerParams(
            collective_id=0, has_side_effects=True, vmem_limit_bytes=60 * 1024 * 1024
        ),
        name="reward_step",
    )(
        latents,
        frame_list,
        reward_scale,
        norm_gain,
        conv_in_weight,
        ln_gain,
        head_vec,
        conv_weight.T,
        patch_weight,
        qkv_weight,
        out_weight,
    )
    spread_rows = grad.reshape(16, 4, 32).transpose(1, 0, 2)
    return (reward.reshape(1), spread_rows.reshape(FR_DEV, ROWS, 32))


def solution(mesh):
    in_specs = (
        P("seq", None, "sp"),
        P(),
        P(),
        P(None, "sp"),
        P(),
        P("seq"),
        P(),
        P(),
        P(None, "sp"),
        P("sp", None),
        P(),
    )
    out_specs = (P("seq"), P("seq", None, "sp"))
    return jax.shard_map(body, mesh=mesh, in_specs=in_specs, out_specs=out_specs, check_vma=False)
```

```python
import functools

import jax
import jax.numpy as jnp
from jax import lax
from jax.experimental import pallas as pl
from jax.experimental.pallas import tpu as pltpu
from jax.sharding import PartitionSpec as P

LAT = 16
CH = 384
VW = 1024
HD = 64
COLS = 8
ROWS = 32
CLIP_FR = 16
FR_DEV = 2
CLIP_DEV = CLIP_FR // FR_DEV
SP = 4
OUT_CH = CH // SP
LOCAL_HEADS = 4
TOKENS = 64
CELLS = ROWS * COLS
HALF = 64
MESH = pl.DeviceIdType.MESH

norm_epsilon = 1e-06
layer_epsilon = 1e-05

f32 = jnp.float32
bf16 = jnp.bfloat16


def dot(left, right):
    return lax.dot_general(left, right, (((1,), (0,)), ((), ())), preferred_element_type=f32)


def dot_last(left, right):
    return lax.dot_general(left, right, (((1,), (1,)), ((), ())), preferred_element_type=f32)


def dot_first(left, right):
    return lax.dot_general(left, right, (((0,), (0,)), ((), ())), preferred_element_type=f32)


def iota(shape, dim):
    return lax.broadcasted_iota(jnp.int32, shape, dim)


def one_hot(condition):
    return jnp.where(condition, 1.0, 0.0).astype(bf16)


def row_mean(value):
    return jnp.sum(value, axis=-1, keepdims=True) * (1.0 / value.shape[-1])


def layer_stats(volume):
    center = row_mean(volume)
    moved = volume - center
    inverse = lax.rsqrt(row_mean(moved * moved) + layer_epsilon)
    return moved * inverse, inverse


def layer_back(whitened, inverse, scaled_grad):
    return inverse * (
        scaled_grad - row_mean(scaled_grad) - whitened * row_mean(scaled_grad * whitened)
    )


def shifted(value, offset):
    if offset == 0:
        return value
    blank = jnp.zeros(value.shape[:-2] + (1, value.shape[-1]), value.dtype)
    if offset > 0:
        return jnp.concatenate([value[..., 1:, :], blank], axis=-2)
    return jnp.concatenate([blank, value[..., :-1, :]], axis=-2)


def moved(value, offset):
    if offset == 0:
        return value
    blank = jnp.zeros((1,) + value.shape[1:], value.dtype)
    if offset > 0:
        return jnp.concatenate([value[1:], blank], axis=0)
    return jnp.concatenate([blank, value[:-1]], axis=0)


def start_copy(source, target, send, recv, device, pending):
    copy = pltpu.make_async_remote_copy(
        src_ref=source,
        dst_ref=target,
        send_sem=send,
        recv_sem=recv,
        device_id=device,
        device_id_type=MESH,
    )
    copy.start()
    pending.append(copy)
    return copy


def exchange(pick, slots, sems, here, place, count, pending):
    copies = {}
    for step in range(1, count):
        peer = lax.rem(here + step, count)
        copies[step] = start_copy(
            pick(step), slots.at[step], sems.at[0, step], sems.at[1, step], place(peer), pending
        )
    return copies


def wait_all(copies):
    for copy in copies.values():
        copy.wait_recv()


def kernel(
    lat_hbm,
    list_hbm,
    scale_hbm,
    gain_hbm,
    wi_hbm,
    ln_hbm,
    head_hbm,
    conv_hbm,
    patch_hbm,
    qkv_hbm,
    out_hbm,
    grad_ref,
    reward_ref,
    lat_ref,
    list_ref,
    scale_ref,
    gain_ref,
    ln_ref,
    head_ref,
    conv_ref,
    patch_ref,
    qkv_ref,
    out_ref,
    wi_pad,
    lat_seq,
    lat_sp,
    z_ref,
    rolled,
    cols,
    first,
    slope,
    act,
    feat,
    embed,
    mix,
    patch_out,
    patch_in,
    lat_back,
    band_out,
    band_in,
    placed,
    clip_out,
    clip_in,
    back_cols,
    load_sem,
    conv_sem,
    patch_sem,
    seq_sems,
    clip_sems,
    lat_sems,
    feat_sems,
    mix_sems,
    patch_sems,
    band_sems,
):
    seq = lax.axis_index("seq")
    sp = lax.axis_index("sp")
    local = lax.rem(seq, CLIP_DEV)
    base = seq - local

    def in_clip(peer):
        return (base + peer, sp)

    def in_band(peer):
        return (seq, peer)

    loads = {}
    pending = []

    def load(name, source, target, sem):
        copy = pltpu.make_async_copy(source, target, sem)
        copy.start()
        loads.setdefault(name, []).append(copy)

    def loaded(*names):
        for name in names:
            for copy in loads.pop(name):
                copy.wait()

    for i, (name, source, target) in enumerate(
        (
            ("lat", lat_hbm, lat_ref),
            ("list", list_hbm, list_ref),
            ("gain", gain_hbm, gain_ref),
            ("wi", wi_hbm, wi_pad.at[0 : 27 * LAT]),
            ("ln", ln_hbm, ln_ref),
            ("head", head_hbm, head_ref),
            ("scale", scale_hbm, scale_ref),
        )
    ):
        load(name, source, target, load_sem.at[i])

    barrier = pltpu.get_barrier_semaphore()
    for step in range(1, CLIP_DEV):
        pl.semaphore_signal(
            barrier,
            inc=1,
            device_id=in_clip(lax.rem(local + step, CLIP_DEV)),
            device_id_type=MESH,
        )
    for step in range(1, SP):
        pl.semaphore_signal(
            barrier, inc=1, device_id=in_band(lax.rem(sp + step, SP)), device_id_type=MESH
        )

    lat_seq[0:2] = jnp.zeros((2, 16, 128), bf16)
    loaded("lat")
    own = lat_ref[...].reshape(FR_DEV * ROWS, 32)
    packed = jnp.zeros((16, 128), f32)
    for j in range(4):
        spot = one_hot(iota((32, 128), 1) == iota((32, 128), 0) + 32 * j)
        packed = packed + dot(own[16 * j : 16 * j + 16], spot)
    lat_seq[pl.ds(2 + local, 1)] = packed.astype(bf16)[None]

    pl.semaphore_wait(barrier, CLIP_DEV - 1 + SP - 1)

    mine = lat_seq.at[pl.ds(2 + local, 1)]
    copies = {}
    for step in range(1, CLIP_DEV):
        copies[step] = start_copy(
            mine,
            mine,
            seq_sems.at[0, step],
            seq_sems.at[1, step],
            in_clip(lax.rem(local + step, CLIP_DEV)),
            pending,
        )

    for dt in range(3):
        for near in range(9):
            load(
                "conv",
                conv_hbm.at[:, CH * (9 * dt + near) : CH * (9 * dt + near + 1)],
                conv_ref.at[OUT_CH * near : OUT_CH * near + OUT_CH, CH * dt : CH * dt + CH],
                conv_sem.at[dt, near],
            )
    for k in range(4):
        for s in range(SP):
            load(
                "patch",
                patch_hbm.at[CH * k + OUT_CH * s : CH * k + OUT_CH * s + OUT_CH],
                patch_ref.at[CH * s + OUT_CH * k : CH * s + OUT_CH * k + OUT_CH],
                patch_sem.at[k, s],
            )
    load("qkv", qkv_hbm, qkv_ref, load_sem.at[7])
    load("out", out_hbm, out_ref, load_sem.at[8])

    wi_pad[27 * LAT :] = jnp.zeros((512 - 27 * LAT, CH), bf16)
    lat_back[...] = jnp.zeros(lat_back.shape, f32)
    placed[...] = jnp.zeros(placed.shape, f32)
    row, col = iota((512, 512), 0), iota((512, 512), 1)
    swap = one_hot(
        ((row >> 7) == ((col >> 5) & 3)) & (((row >> 5) & 3) == (col >> 7)) & ((row & 31) == (col & 31))
    )
    row, col = iota((256, 256), 0), iota((256, 256), 1)
    kind, token = row >> 6, row & 63
    to_patch = one_hot(
        col == (2 * (token >> 4) + (kind & 1)) * ROWS + 2 * (token & 15) + (kind >> 1)
    )
    own_channels = one_hot(iota((CH, OUT_CH), 0) == iota((CH, OUT_CH), 1) + sp * OUT_CH)

    wait_all(copies)

    loaded("list")
    where = lax.rem(list_ref[seq], CLIP_FR)
    chunk, odd = lax.div(where, 2), lax.rem(where, 2)
    lat_sp[pl.ds(sp, 1)] = lat_seq[pl.ds(chunk, 3)].reshape(1, 48, 128)
    copies = {}
    for step in range(1, SP):
        copies[step] = start_copy(
            lat_sp.at[sp],
            lat_sp.at[sp],
            lat_sems.at[0, step],
            lat_sems.at[1, step],
            in_band(lax.rem(sp + step, SP)),
            pending,
        )
    wait_all(copies)
    wide = jnp.concatenate([lat_sp[s] for s in range(SP)], axis=1)
    spots = dot(wide, swap)
    for c in range(3):
        for j in range(4):
            z_ref[2 * c + j // 2, 16 * (j % 2) : 16 * (j % 2) + 16] = spots[
                16 * c : 16 * c + 16, 128 * j : 128 * j + 128
            ]
    z = z_ref[pl.ds(odd, 5)]
    taps = jnp.stack([shifted(z, dr - 1) for dr in range(3)], axis=1).reshape(480, 128)
    for k in range(8):
        rolled[k] = (taps if k == 0 else pltpu.roll(taps, 16 * k, 1)).reshape(15, ROWS, 128)

    lane = iota((ROWS, 128), 1)
    pieces = []
    for block in range(4):
        inner = lax.rem(lane + 128 * block, 48) >> 4
        taps_here = [t for t in range(9) if 48 * t < 128 * block + 128 and 48 * t + 48 > 128 * block]
        pieces.append((inner, taps_here))

    def inside(inner, c):
        return ((inner > 0) | (c > 0)) & ((inner < 2) | (c < COLS - 1))

    def build(c, carry):
        for frame in range(3):
            for block, (inner, taps_here) in enumerate(pieces):
                value = None
                for tap in taps_here:
                    part = rolled[lax.rem(3 * tap + 9 - c, 8), 3 * frame + tap]
                    begin = 48 * tap - 128 * block
                    value = part if value is None else jnp.where(lane >= begin, part, value)
                cols[frame, c, :, 128 * block : 128 * block + 128] = jnp.where(
                    inside(inner, c), value, 0.0
                ).astype(bf16)
        return carry

    lax.fori_loop(0, COLS, build, 0, unroll=True)

    loaded("gain", "wi")
    gain = gain_ref[...].reshape(1, CH)
    for frame in range(3):
        spots = dot(cols[frame].reshape(CELLS, 512), wi_pad[...])
        first[frame] = spots.astype(bf16)

    for frame in range(3):
        for half_frame in range(2):
            rows = slice(128 * half_frame, 128 * half_frame + 128)
            h = first[frame, rows].astype(f32)
            unit = h * lax.rsqrt(row_mean(h * h) + norm_epsilon) * gain
            act[rows, CH * frame : CH * frame + CH] = (unit * jax.nn.sigmoid(unit)).astype(bf16)

    loaded("conv")
    spots = dot_last(act[...], conv_ref[...])
    total = dot(first[2], own_channels).reshape(COLS, ROWS, OUT_CH)
    for dr in range(3):
        line = None
        for dc in range(3):
            start = OUT_CH * (3 * dr + dc)
            term = moved(spots[:, start : start + OUT_CH].reshape(COLS, ROWS, OUT_CH), dc - 1)
            line = term if line is None else line + term
        total = total + shifted(line, dr - 1)
    patches = dot(to_patch, total.reshape(CELLS, OUT_CH).astype(bf16))
    feat[0] = jnp.concatenate(
        [patches[TOKENS * k : TOKENS * k + TOKENS] for k in range(4)], axis=1
    ).astype(bf16)

    copies = exchange(
        lambda step: feat.at[0], feat, feat_sems, sp, in_band, SP, pending
    )
    loaded("patch")

    def embed_from(step):
        source = lax.rem(sp + SP - step, SP)
        rows = pl.ds(pl.multiple_of(source * CH, 128), CH)
        embed[pl.ds(source, 1)] = dot(feat[step], patch_ref[rows, :])[None]

    embed_from(0)
    for frame in range(3):
        h = first[frame].astype(f32)
        inverse = lax.rsqrt(row_mean(h * h) + norm_epsilon)
        unit = h * inverse * gain
        gate = jax.nn.sigmoid(unit)
        slope[frame] = gate * (1.0 + unit * (1.0 - gate)) * (gain * inverse)
    for step in (1, 3, 2):
        copies[step].wait_recv()
        embed_from(step)
    loaded("ln", "qkv", "out", "head", "scale")

    x = embed[0]
    for s in range(1, SP):
        x = x + embed[s]
    x = x.astype(bf16).astype(f32)
    white_in, inverse_in = layer_stats(x)
    gain_in, gain_out = ln_ref[0:1], ln_ref[1:2]
    qkv = dot((white_in * gain_in).astype(bf16), qkv_ref[...]).astype(bf16)
    heads = []
    mixed = []
    for head in range(LOCAL_HEADS):
        start = 3 * HD * head
        q, k, v = (qkv[:, start + HD * i : start + HD * i + HD] for i in range(3))
        scores = dot_last(q, k) * (HD**-0.5)
        weights = jnp.exp(scores - jnp.max(scores, axis=-1, keepdims=True))
        probs = weights / jnp.sum(weights, axis=-1, keepdims=True)
        probs_low = probs.astype(bf16)
        mixed.append(dot(probs_low, v).astype(bf16))
        heads.append((q, k, v, probs, probs_low))
    mix[pl.ds(sp, 1)] = dot(jnp.concatenate(mixed, axis=1), out_ref[...]).astype(bf16)[None]

    copies = {}
    for step in range(1, SP):
        copies[step] = start_copy(
            mix.at[sp],
            mix.at[sp],
            mix_sems.at[0, step],
            mix_sems.at[1, step],
            in_band(lax.rem(sp + step, SP)),
            pending,
        )
    wait_all(copies)

    attended = mix[0].astype(f32)
    for s in range(1, SP):
        attended = attended + mix[s].astype(f32)
    y = x + attended
    white_out, inverse_out = layer_stats(y)
    vector = head_ref[...].reshape(1, VW)
    reward = jnp.sum(white_out * gain_out * vector, axis=1, keepdims=True)
    reward_ref[...] = jnp.sum(reward, axis=0, keepdims=True) * (1.0 / TOKENS)
    scaled = (scale_ref[0] * (1.0 / TOKENS)) * vector * gain_out
    dy = layer_back(white_out, inverse_out, jnp.broadcast_to(scaled, y.shape))
    do = dot_last(dy.astype(bf16), out_ref[...]).astype(bf16)
    grads = []
    for head in range(LOCAL_HEADS):
        q, k, v, probs, probs_low = heads[head]
        d_out = do[:, HD * head : HD * head + HD]
        d_probs = dot_last(d_out, v)
        d_scores = (
            probs
            * (d_probs - jnp.sum(d_probs * probs, axis=-1, keepdims=True))
            * (HD**-0.5)
        ).astype(bf16)
        grads.append(dot(d_scores, k).astype(bf16))
        grads.append(dot_first(d_scores, q).astype(bf16))
        grads.append(dot_first(probs_low, d_out).astype(bf16))
    da = dot_last(jnp.concatenate(grads, axis=1), qkv_ref[...])
    dx = layer_back(white_in, inverse_in, da * gain_in) + dy * (1.0 / SP)
    dx_low = dx.astype(bf16)
    copies = {}
    for step in (2, 1, 3, 0):
        peer = lax.rem(sp + step, SP)
        rows = pl.ds(pl.multiple_of(peer * CH, 128), CH)
        block = dot_last(dx_low, patch_ref[rows, :]).astype(bf16)
        if step == 0:
            patch_in[0] = block
        else:
            patch_out[step] = block
            copies[step] = start_copy(
                patch_out.at[step],
                patch_in.at[step],
                patch_sems.at[0, step],
                patch_sems.at[1, step],
                in_band(peer),
                pending,
            )

    wait_all(copies)

    summed = patch_in[0].astype(f32)
    for s in range(1, SP):
        summed = summed + patch_in[s].astype(f32)
    summed = jnp.concatenate(
        [summed[:, OUT_CH * k : OUT_CH * k + OUT_CH] for k in range(4)], axis=0
    )
    d_feat = dot_first(to_patch, summed.astype(bf16))
    d_cells = d_feat.reshape(COLS, ROWS, OUT_CH)
    lines = [shifted(d_cells, 1 - dr).astype(bf16) for dr in range(3)]
    spread_out = jnp.concatenate(
        [
            moved(lines[dr], 1 - dc).reshape(CELLS, OUT_CH)
            for dr in range(3)
            for dc in range(3)
        ],
        axis=1,
    )
    d_own = dot_last(d_feat.astype(bf16), own_channels)

    for frame in (2, 1, 0):
        d_act = dot(spread_out, conv_ref[:, CH * frame : CH * frame + CH])
        h = first[frame].astype(f32)
        square = row_mean(h * h) + norm_epsilon
        d_unit = d_act * slope[frame]
        d_first = d_unit - h * (row_mean(d_unit * h) / square)
        if frame == 2:
            d_first = d_first + d_own
        back_cols[frame] = dot_last(d_first.astype(bf16), wi_pad[...]).reshape(COLS, ROWS, 512)

    def collect(c, carry):
        totals = list(carry)
        for frame in range(3):
            for block, (inner, taps_here) in enumerate(pieces):
                value = jnp.where(
                    inside(inner, c), back_cols[frame, c, :, 128 * block : 128 * block + 128], 0.0
                )
                for tap in taps_here:
                    begin = 48 * tap - 128 * block
                    within = value
                    if begin > 0:
                        within = jnp.where(lane >= begin, within, 0.0)
                    if begin + 48 < 128:
                        within = jnp.where(lane < begin + 48, within, 0.0)
                    turn = lax.rem(16 * (c + 23 - 3 * tap + 8), 128)
                    totals[3 * frame + tap] = totals[3 * frame + tap] + pltpu.roll(within, turn, 1)
        return tuple(totals)

    gathered = lax.fori_loop(
        0, COLS, collect, tuple(jnp.zeros((ROWS, 128), f32) for _ in range(15)), unroll=True
    )
    gathered = jnp.stack(gathered, axis=0)
    gathered = gathered.reshape(5, 3, ROWS, 128)
    lat_back[1:6] = (
        gathered[:, 1] + shifted(gathered[:, 0], 1) + shifted(gathered[:, 2], -1)
    )
    aligned = lat_back[pl.ds(1 - odd, 6)].astype(bf16)
    wide = jnp.concatenate(
        [
            jnp.concatenate(
                [aligned[2 * c + j // 2, 16 * (j % 2) : 16 * (j % 2) + 16] for j in range(4)], axis=1
            )
            for c in range(3)
        ],
        axis=0,
    )
    bands = dot(wide, swap).astype(bf16)
    for s in range(SP):
        band_out[s] = bands[:, 128 * s : 128 * s + 128]

    copies = exchange(
        lambda step: band_out.at[lax.rem(sp + step, SP)],
        band_in,
        band_sems,
        sp,
        in_band,
        SP,
        pending,
    )
    band_in[pl.ds(0, 1)] = band_out[pl.ds(sp, 1)]
    wait_all(copies)

    summed = band_in[0].astype(f32)
    for s in range(1, SP):
        summed = summed + band_in[s].astype(f32)
    placed[5:8] = summed.reshape(3, 16, 128)
    clip_out[...] = placed[pl.ds(7 - chunk, 8)].astype(bf16)
    copies = exchange(
        lambda step: clip_out.at[lax.rem(local + step, CLIP_DEV)],
        clip_in,
        clip_sems,
        local,
        in_clip,
        CLIP_DEV,
        pending,
    )
    clip_in[pl.ds(0, 1)] = clip_out[pl.ds(local, 1)]
    wait_all(copies)

    summed = clip_in[0].astype(f32)
    for s in range(1, CLIP_DEV):
        summed = summed + clip_in[s].astype(f32)
    for j in range(4):
        grad_ref[j // 2, 16 * (j % 2) : 16 * (j % 2) + 16] = summed[:, 32 * j : 32 * j + 32]
    for copy in pending:
        copy.wait_send()


def body(
    latents,
    conv_in_weight,
    norm_gain,
    conv_weight,
    frame_list,
    reward_scale,
    patch_weight,
    ln_gain,
    qkv_weight,
    out_weight,
    head_vec,
):
    vmem = pl.BlockSpec(memory_space=pltpu.VMEM)
    hbm = pl.BlockSpec(memory_space=pltpu.HBM)
    grad, reward = pl.pallas_call(
        kernel,
        out_shape=(
            jax.ShapeDtypeStruct((FR_DEV, ROWS, 32), f32),
            jax.ShapeDtypeStruct((1, 1), f32),
        ),
        in_specs=[hbm] * 11,
        out_specs=(vmem, vmem),
        scratch_shapes=[
            pltpu.VMEM((FR_DEV, ROWS, 32), bf16),
            pltpu.SMEM((64,), jnp.int32),
            pltpu.SMEM((1,), f32),
            pltpu.VMEM((CH,), f32),
            pltpu.VMEM((2, VW), f32),
            pltpu.VMEM((VW,), f32),
            pltpu.VMEM((9 * OUT_CH, 3 * CH), bf16),
            pltpu.VMEM((4 * CH, VW), bf16),
            pltpu.VMEM((VW, 3 * HD * LOCAL_HEADS), bf16),
            pltpu.VMEM((HD * LOCAL_HEADS, VW), bf16),
            pltpu.VMEM((512, CH), bf16),
            pltpu.VMEM((2 + CLIP_DEV, 16, 128), bf16),
            pltpu.VMEM((SP, 48, 128), bf16),
            pltpu.VMEM((6, ROWS, 128), f32),
            pltpu.VMEM((8, 15, ROWS, 128), f32),
            pltpu.VMEM((3, COLS, ROWS, 512), bf16),
            pltpu.VMEM((3, CELLS, CH), bf16),
            pltpu.VMEM((3, CELLS, CH), f32),
            pltpu.VMEM((CELLS, 3 * CH), bf16),
            pltpu.VMEM((SP, TOKENS, CH), bf16),
            pltpu.VMEM((SP, TOKENS, VW), f32),
            pltpu.VMEM((SP, TOKENS, VW), bf16),
            pltpu.VMEM((SP, TOKENS, CH), bf16),
            pltpu.VMEM((SP, TOKENS, CH), bf16),
            pltpu.VMEM((7, ROWS, 128), f32),
            pltpu.VMEM((SP, 48, 128), bf16),
            pltpu.VMEM((SP, 48, 128), bf16),
            pltpu.VMEM((15, 16, 128), f32),
            pltpu.VMEM((CLIP_DEV, 16, 128), bf16),
            pltpu.VMEM((CLIP_DEV, 16, 128), bf16),
            pltpu.VMEM((3, COLS, ROWS, 512), f32),
            pltpu.SemaphoreType.DMA((9,)),
            pltpu.SemaphoreType.DMA((3, 9)),
            pltpu.SemaphoreType.DMA((4, SP)),
            pltpu.SemaphoreType.DMA((2, CLIP_DEV)),
            pltpu.SemaphoreType.DMA((2, CLIP_DEV)),
        ]
        + [pltpu.SemaphoreType.DMA((2, SP))] * 5,
        compiler_params=pltpu.CompilerParams(
            collective_id=0, has_side_effects=True, vmem_limit_bytes=60 * 1024 * 1024
        ),
        name="reward_step",
    )(
        latents,
        frame_list,
        reward_scale,
        norm_gain,
        conv_in_weight,
        ln_gain,
        head_vec,
        conv_weight.T,
        patch_weight,
        qkv_weight,
        out_weight,
    )
    return (reward.reshape(1), grad)


def solution(mesh):
    in_specs = (
        P("seq", None, "sp"),
        P(),
        P(),
        P(None, "sp"),
        P(),
        P("seq"),
        P(),
        P(),
        P(None, "sp"),
        P("sp", None),
        P(),
    )
    out_specs = (P("seq"), P("seq", None, "sp"))
    return jax.shard_map(body, mesh=mesh, in_specs=in_specs, out_specs=out_specs, check_vma=False)
```

```python
import functools

import jax
import jax.numpy as jnp
from jax import lax
from jax.experimental import pallas as pl
from jax.experimental.pallas import tpu as pltpu
from jax.sharding import PartitionSpec as P

LAT = 16
CH = 384
VW = 1024
HD = 64
COLS = 8
ROWS = 32
CLIP_FR = 16
FR_DEV = 2
CLIP_DEV = CLIP_FR // FR_DEV
SP = 4
OUT_CH = CH // SP
LOCAL_HEADS = 4
TOKENS = 64
CELLS = ROWS * COLS
HALF = 64
MESH = pl.DeviceIdType.MESH

norm_epsilon = 1e-06
layer_epsilon = 1e-05

f32 = jnp.float32
bf16 = jnp.bfloat16


def dot(left, right):
    return lax.dot_general(left, right, (((1,), (0,)), ((), ())), preferred_element_type=f32)


def dot_last(left, right):
    return lax.dot_general(left, right, (((1,), (1,)), ((), ())), preferred_element_type=f32)


def dot_first(left, right):
    return lax.dot_general(left, right, (((0,), (0,)), ((), ())), preferred_element_type=f32)


def iota(shape, dim):
    return lax.broadcasted_iota(jnp.int32, shape, dim)


def one_hot(condition):
    return jnp.where(condition, 1.0, 0.0).astype(bf16)


def row_mean(value):
    return jnp.sum(value, axis=-1, keepdims=True) * (1.0 / value.shape[-1])


def layer_stats(volume):
    center = row_mean(volume)
    moved = volume - center
    inverse = lax.rsqrt(row_mean(moved * moved) + layer_epsilon)
    return moved * inverse, inverse


def layer_back(whitened, inverse, scaled_grad):
    return inverse * (
        scaled_grad - row_mean(scaled_grad) - whitened * row_mean(scaled_grad * whitened)
    )


def shifted(value, offset):
    if offset == 0:
        return value
    blank = jnp.zeros(value.shape[:-2] + (1, value.shape[-1]), value.dtype)
    if offset > 0:
        return jnp.concatenate([value[..., 1:, :], blank], axis=-2)
    return jnp.concatenate([blank, value[..., :-1, :]], axis=-2)


def moved(value, offset):
    if offset == 0:
        return value
    blank = jnp.zeros((1,) + value.shape[1:], value.dtype)
    if offset > 0:
        return jnp.concatenate([value[1:], blank], axis=0)
    return jnp.concatenate([blank, value[:-1]], axis=0)


def start_copy(source, target, send, recv, device, pending):
    copy = pltpu.make_async_remote_copy(
        src_ref=source,
        dst_ref=target,
        send_sem=send,
        recv_sem=recv,
        device_id=device,
        device_id_type=MESH,
    )
    copy.start()
    pending.append(copy)
    return copy


def exchange(pick, slots, sems, here, place, count, pending):
    copies = {}
    for step in sorted(range(1, count), key=lambda d: -min(d, count - d)):
        peer = lax.rem(here + step, count)
        copies[step] = start_copy(
            pick(step), slots.at[step], sems.at[0, step], sems.at[1, step], place(peer), pending
        )
    return copies


def wait_all(copies):
    for copy in copies.values():
        copy.wait_recv()


def kernel(
    lat_hbm,
    list_hbm,
    scale_hbm,
    gain_hbm,
    wi_hbm,
    ln_hbm,
    head_hbm,
    conv_hbm,
    patch_hbm,
    qkv_hbm,
    out_hbm,
    clip_in,
    reward_hbm,
    lat_ref,
    list_ref,
    scale_ref,
    gain_ref,
    ln_ref,
    head_ref,
    conv_ref,
    patch_ref,
    qkv_ref,
    out_ref,
    wi_pad,
    lat_seq,
    lat_sp,
    z_ref,
    rolled,
    cols,
    first,
    slope,
    act,
    feat,
    embed,
    mix,
    patch_out,
    patch_in,
    lat_back,
    band_out,
    band_in,
    placed,
    clip_out,
    reward_ref,
    back_cols,
    load_sem,
    conv_sem,
    patch_sem,
    seq_sems,
    clip_sems,
    lat_sems,
    feat_sems,
    mix_sems,
    patch_sems,
    band_sems,
):
    seq = lax.axis_index("seq")
    sp = lax.axis_index("sp")
    local = lax.rem(seq, CLIP_DEV)
    base = seq - local

    def in_clip(peer):
        return (base + peer, sp)

    def in_band(peer):
        return (seq, peer)

    barrier = pltpu.get_barrier_semaphore()
    for step in range(1, CLIP_DEV):
        pl.semaphore_signal(
            barrier,
            inc=1,
            device_id=in_clip(lax.rem(local + step, CLIP_DEV)),
            device_id_type=MESH,
        )
    for step in range(1, SP):
        pl.semaphore_signal(
            barrier, inc=1, device_id=in_band(lax.rem(sp + step, SP)), device_id_type=MESH
        )

    loads = {}
    pending = []

    def load(name, source, target, sem):
        copy = pltpu.make_async_copy(source, target, sem)
        copy.start()
        loads.setdefault(name, []).append(copy)

    def loaded(*names):
        for name in names:
            for copy in loads.pop(name):
                copy.wait()

    for i, (name, source, target) in enumerate(
        (
            ("lat", lat_hbm, lat_ref),
            ("list", list_hbm, list_ref),
            ("gain", gain_hbm, gain_ref),
            ("wi", wi_hbm, wi_pad.at[0 : 27 * LAT]),
            ("ln", ln_hbm, ln_ref),
            ("head", head_hbm, head_ref),
            ("scale", scale_hbm, scale_ref),
        )
    ):
        load(name, source, target, load_sem.at[i])

    lat_seq[0:2] = jnp.zeros((2, 16, 128), bf16)
    loaded("lat")
    own = lat_ref[...].reshape(FR_DEV * ROWS, 32)
    packed = jnp.zeros((16, 128), f32)
    for j in range(4):
        spot = one_hot(iota((32, 128), 1) == iota((32, 128), 0) + 32 * j)
        packed = packed + dot(own[16 * j : 16 * j + 16], spot)
    lat_seq[pl.ds(2 + local, 1)] = packed.astype(bf16)[None]

    pl.semaphore_wait(barrier, CLIP_DEV - 1 + SP - 1)

    mine = lat_seq.at[pl.ds(2 + local, 1)]
    copies = {}
    for step in range(1, CLIP_DEV):
        copies[step] = start_copy(
            mine,
            mine,
            seq_sems.at[0, step],
            seq_sems.at[1, step],
            in_clip(lax.rem(local + step, CLIP_DEV)),
            pending,
        )

    for dt in range(3):
        for near in range(9):
            load(
                "conv",
                conv_hbm.at[:, CH * (9 * dt + near) : CH * (9 * dt + near + 1)],
                conv_ref.at[OUT_CH * near : OUT_CH * near + OUT_CH, CH * dt : CH * dt + CH],
                conv_sem.at[dt, near],
            )
    for k in range(4):
        for s in range(SP):
            load(
                "patch",
                patch_hbm.at[CH * k + OUT_CH * s : CH * k + OUT_CH * s + OUT_CH],
                patch_ref.at[CH * s + OUT_CH * k : CH * s + OUT_CH * k + OUT_CH],
                patch_sem.at[k, s],
            )
    load("qkv", qkv_hbm, qkv_ref, load_sem.at[7])
    load("out", out_hbm, out_ref, load_sem.at[8])

    wi_pad[27 * LAT :] = jnp.zeros((512 - 27 * LAT, CH), bf16)
    lat_back[...] = jnp.zeros(lat_back.shape, f32)
    placed[...] = jnp.zeros(placed.shape, f32)
    row, col = iota((512, 512), 0), iota((512, 512), 1)
    swap = one_hot(
        ((row >> 7) == ((col >> 5) & 3)) & (((row >> 5) & 3) == (col >> 7)) & ((row & 31) == (col & 31))
    )
    row, col = iota((256, 256), 0), iota((256, 256), 1)
    kind, token = row >> 6, row & 63
    to_patch = one_hot(
        col == (2 * (token >> 4) + (kind & 1)) * ROWS + 2 * (token & 15) + (kind >> 1)
    )
    own_channels = one_hot(iota((CH, OUT_CH), 0) == iota((CH, OUT_CH), 1) + sp * OUT_CH)

    wait_all(copies)

    loaded("list")
    where = lax.rem(list_ref[seq], CLIP_FR)
    chunk, odd = lax.div(where, 2), lax.rem(where, 2)
    lat_sp[pl.ds(sp, 1)] = lat_seq[pl.ds(chunk, 3)].reshape(1, 48, 128)
    copies = {}
    for step in (2, 1, 3):
        copies[step] = start_copy(
            lat_sp.at[sp],
            lat_sp.at[sp],
            lat_sems.at[0, step],
            lat_sems.at[1, step],
            in_band(lax.rem(sp + step, SP)),
            pending,
        )
    wait_all(copies)
    wide = jnp.concatenate([lat_sp[s] for s in range(SP)], axis=1)
    spots = dot(wide, swap)
    for c in range(3):
        for j in range(4):
            z_ref[2 * c + j // 2, 16 * (j % 2) : 16 * (j % 2) + 16] = spots[
                16 * c : 16 * c + 16, 128 * j : 128 * j + 128
            ]
    z = z_ref[pl.ds(odd, 5)]
    taps = jnp.stack([shifted(z, dr - 1) for dr in range(3)], axis=1).reshape(480, 128)
    for k in range(8):
        rolled[k] = (taps if k == 0 else pltpu.roll(taps, 16 * k, 1)).reshape(15, ROWS, 128)

    lane = iota((ROWS, 128), 1)
    pieces = []
    for block in range(4):
        inner = lax.rem(lane + 128 * block, 48) >> 4
        taps_here = [t for t in range(9) if 48 * t < 128 * block + 128 and 48 * t + 48 > 128 * block]
        pieces.append((inner, taps_here))

    def inside(inner, c):
        return ((inner > 0) | (c > 0)) & ((inner < 2) | (c < COLS - 1))

    def build(c, carry):
        for frame in range(3):
            for block, (inner, taps_here) in enumerate(pieces):
                value = None
                for tap in taps_here:
                    part = rolled[lax.rem(3 * tap + 9 - c, 8), 3 * frame + tap]
                    begin = 48 * tap - 128 * block
                    value = part if value is None else jnp.where(lane >= begin, part, value)
                cols[frame, c, :, 128 * block : 128 * block + 128] = jnp.where(
                    inside(inner, c), value, 0.0
                ).astype(bf16)
        return carry

    lax.fori_loop(0, COLS, build, 0, unroll=True)

    loaded("gain", "wi")
    gain = gain_ref[...].reshape(1, CH)
    for frame in range(3):
        spots = dot(cols[frame].reshape(CELLS, 512), wi_pad[...])
        first[frame] = spots.astype(bf16)

    for frame in range(3):
        for half_frame in range(2):
            rows = slice(128 * half_frame, 128 * half_frame + 128)
            h = first[frame, rows].astype(f32)
            unit = h * lax.rsqrt(row_mean(h * h) + norm_epsilon) * gain
            act[rows, CH * frame : CH * frame + CH] = (unit * jax.nn.sigmoid(unit)).astype(bf16)

    loaded("conv")
    spots = dot_last(act[...], conv_ref[...])
    total = dot(first[2], own_channels).reshape(COLS, ROWS, OUT_CH)
    for dr in range(3):
        line = None
        for dc in range(3):
            start = OUT_CH * (3 * dr + dc)
            term = moved(spots[:, start : start + OUT_CH].reshape(COLS, ROWS, OUT_CH), dc - 1)
            line = term if line is None else line + term
        total = total + shifted(line, dr - 1)
    patches = dot(to_patch, total.reshape(CELLS, OUT_CH).astype(bf16))
    feat[0] = jnp.concatenate(
        [patches[TOKENS * k : TOKENS * k + TOKENS] for k in range(4)], axis=1
    ).astype(bf16)

    copies = exchange(
        lambda step: feat.at[0], feat, feat_sems, sp, in_band, SP, pending
    )
    loaded("patch")

    def embed_from(step):
        source = lax.rem(sp + SP - step, SP)
        rows = pl.ds(pl.multiple_of(source * CH, 128), CH)
        embed[pl.ds(source, 1)] = dot(feat[step], patch_ref[rows, :])[None]

    embed_from(0)
    for frame in range(3):
        h = first[frame].astype(f32)
        inverse = lax.rsqrt(row_mean(h * h) + norm_epsilon)
        unit = h * inverse * gain
        gate = jax.nn.sigmoid(unit)
        slope[frame] = gate * (1.0 + unit * (1.0 - gate)) * (gain * inverse)
    for step in (1, 3, 2):
        copies[step].wait_recv()
        embed_from(step)
    loaded("ln", "qkv", "out", "head", "scale")

    x = embed[0]
    for s in range(1, SP):
        x = x + embed[s]
    x = x.astype(bf16).astype(f32)
    white_in, inverse_in = layer_stats(x)
    gain_in, gain_out = ln_ref[0:1], ln_ref[1:2]
    qkv = dot((white_in * gain_in).astype(bf16), qkv_ref[...]).astype(bf16)
    heads = range(LOCAL_HEADS)

    def part_of(i):
        return [qkv[:, HD * (3 * h + i) : HD * (3 * h + i) + HD] for h in heads]

    def rows_of(stacked):
        return [stacked[TOKENS * h : TOKENS * h + TOKENS] for h in heads]

    query, key, value = part_of(0), part_of(1), part_of(2)
    scores = jnp.concatenate([dot_last(query[h], key[h]) for h in heads], axis=0) * (HD**-0.5)
    weights = jnp.exp(scores - jnp.max(scores, axis=-1, keepdims=True))
    probs = weights / jnp.sum(weights, axis=-1, keepdims=True)
    probs_low = rows_of(probs.astype(bf16))
    mixed = [dot(probs_low[h], value[h]).astype(bf16) for h in heads]
    mix[pl.ds(sp, 1)] = dot(jnp.concatenate(mixed, axis=1), out_ref[...]).astype(bf16)[None]

    copies = {}
    for step in (2, 1, 3):
        copies[step] = start_copy(
            mix.at[sp],
            mix.at[sp],
            mix_sems.at[0, step],
            mix_sems.at[1, step],
            in_band(lax.rem(sp + step, SP)),
            pending,
        )
    wait_all(copies)

    attended = mix[0].astype(f32)
    for s in range(1, SP):
        attended = attended + mix[s].astype(f32)
    y = x + attended
    white_out, inverse_out = layer_stats(y)
    vector = head_ref[...].reshape(1, VW)
    reward = jnp.sum(white_out * gain_out * vector, axis=1, keepdims=True)
    reward_ref[...] = jnp.broadcast_to(
        jnp.sum(reward, axis=0, keepdims=True) * (1.0 / TOKENS), (8, 128)
    )
    load("reward", reward_ref, reward_hbm, load_sem.at[9])
    scaled = (scale_ref[0] * (1.0 / TOKENS)) * vector * gain_out
    dy = layer_back(white_out, inverse_out, jnp.broadcast_to(scaled, y.shape))
    do = dot_last(dy.astype(bf16), out_ref[...]).astype(bf16)
    d_out = [do[:, HD * h : HD * h + HD] for h in heads]
    d_probs = jnp.concatenate([dot_last(d_out[h], value[h]) for h in heads], axis=0)
    d_scores = probs * (d_probs - jnp.sum(d_probs * probs, axis=-1, keepdims=True)) * (HD**-0.5)
    d_scores = rows_of(d_scores.astype(bf16))
    grads = []
    for h in heads:
        grads.append(dot(d_scores[h], key[h]).astype(bf16))
        grads.append(dot_first(d_scores[h], query[h]).astype(bf16))
        grads.append(dot_first(probs_low[h], d_out[h]).astype(bf16))
    da = dot_last(jnp.concatenate(grads, axis=1), qkv_ref[...])
    dx = layer_back(white_in, inverse_in, da * gain_in) + dy * (1.0 / SP)
    dx_low = dx.astype(bf16)
    copies = {}
    for step in (2, 1, 3, 0):
        peer = lax.rem(sp + step, SP)
        rows = pl.ds(pl.multiple_of(peer * CH, 128), CH)
        block = dot_last(dx_low, patch_ref[rows, :]).astype(bf16)
        if step == 0:
            patch_in[0] = block
        else:
            patch_out[step] = block
            copies[step] = start_copy(
                patch_out.at[step],
                patch_in.at[step],
                patch_sems.at[0, step],
                patch_sems.at[1, step],
                in_band(peer),
                pending,
            )

    wait_all(copies)

    summed = patch_in[0].astype(f32)
    for s in range(1, SP):
        summed = summed + patch_in[s].astype(f32)
    summed = jnp.concatenate(
        [summed[:, OUT_CH * k : OUT_CH * k + OUT_CH] for k in range(4)], axis=0
    )
    d_feat = dot_first(to_patch, summed.astype(bf16))
    d_cells = d_feat.reshape(COLS, ROWS, OUT_CH)
    lines = [shifted(d_cells, 1 - dr).astype(bf16) for dr in range(3)]
    spread_out = jnp.concatenate(
        [
            moved(lines[dr], 1 - dc).reshape(CELLS, OUT_CH)
            for dr in range(3)
            for dc in range(3)
        ],
        axis=1,
    )
    d_own = dot_last(d_feat.astype(bf16), own_channels)

    for frame in (2, 1, 0):
        d_act = dot(spread_out, conv_ref[:, CH * frame : CH * frame + CH])
        h = first[frame].astype(f32)
        square = row_mean(h * h) + norm_epsilon
        d_unit = d_act * slope[frame]
        d_first = d_unit - h * (row_mean(d_unit * h) / square)
        if frame == 2:
            d_first = d_first + d_own
        back_cols[frame] = dot_last(d_first.astype(bf16), wi_pad[...]).reshape(COLS, ROWS, 512)

    def collect(c, carry):
        totals = list(carry)
        for frame in range(3):
            for block, (inner, taps_here) in enumerate(pieces):
                value = jnp.where(
                    inside(inner, c), back_cols[frame, c, :, 128 * block : 128 * block + 128], 0.0
                )
                for tap in taps_here:
                    begin = 48 * tap - 128 * block
                    within = value
                    if begin > 0:
                        within = jnp.where(lane >= begin, within, 0.0)
                    if begin + 48 < 128:
                        within = jnp.where(lane < begin + 48, within, 0.0)
                    turn = lax.rem(16 * (c + 23 - 3 * tap + 8), 128)
                    totals[3 * frame + tap] = totals[3 * frame + tap] + pltpu.roll(within, turn, 1)
        return tuple(totals)

    gathered = lax.fori_loop(
        0, COLS, collect, tuple(jnp.zeros((ROWS, 128), f32) for _ in range(15)), unroll=True
    )
    gathered = jnp.stack(gathered, axis=0)
    gathered = gathered.reshape(5, 3, ROWS, 128)
    lat_back[1:6] = (
        gathered[:, 1] + shifted(gathered[:, 0], 1) + shifted(gathered[:, 2], -1)
    )
    aligned = lat_back[pl.ds(1 - odd, 6)].astype(bf16)
    wide = jnp.concatenate(
        [
            jnp.concatenate(
                [aligned[2 * c + j // 2, 16 * (j % 2) : 16 * (j % 2) + 16] for j in range(4)], axis=1
            )
            for c in range(3)
        ],
        axis=0,
    )
    bands = dot(wide, swap).astype(bf16)
    for s in range(SP):
        band_out[s] = bands[:, 128 * s : 128 * s + 128]

    copies = exchange(
        lambda step: band_out.at[lax.rem(sp + step, SP)],
        band_in,
        band_sems,
        sp,
        in_band,
        SP,
        pending,
    )
    band_in[pl.ds(0, 1)] = band_out[pl.ds(sp, 1)]
    wait_all(copies)

    summed = band_in[0].astype(f32)
    for s in range(1, SP):
        summed = summed + band_in[s].astype(f32)
    placed[5:8] = summed.reshape(3, 16, 128)
    clip_out[...] = placed[pl.ds(7 - chunk, 8)].astype(bf16)
    copies = exchange(
        lambda step: clip_out.at[lax.rem(local + step, CLIP_DEV)],
        clip_in,
        clip_sems,
        local,
        in_clip,
        CLIP_DEV,
        pending,
    )
    load("clip", clip_out.at[pl.ds(local, 1)], clip_in.at[0:1], load_sem.at[10])
    wait_all(copies)

    loaded("clip", "reward")
    for copy in pending:
        copy.wait_send()


def finish(clip_in, reward_in, reward_ref, grad_ref):
    summed = clip_in[0].astype(f32)
    for s in range(1, CLIP_DEV):
        summed = summed + clip_in[s].astype(f32)
    for j in range(4):
        grad_ref[j // 2, 16 * (j % 2) : 16 * (j % 2) + 16] = summed[:, 32 * j : 32 * j + 32]
    reward_ref[...] = reward_in[0:1, 0:1]


def body(
    latents,
    conv_in_weight,
    norm_gain,
    conv_weight,
    frame_list,
    reward_scale,
    patch_weight,
    ln_gain,
    qkv_weight,
    out_weight,
    head_vec,
):
    vmem = pl.BlockSpec(memory_space=pltpu.VMEM)
    hbm = pl.BlockSpec(memory_space=pltpu.HBM)
    parts, rewards = pl.pallas_call(
        kernel,
        out_shape=(
            jax.ShapeDtypeStruct((CLIP_DEV, 16, 128), bf16),
            jax.ShapeDtypeStruct((8, 128), f32),
        ),
        in_specs=[hbm] * 11,
        out_specs=(hbm, hbm),
        scratch_shapes=[
            pltpu.VMEM((FR_DEV, ROWS, 32), bf16),
            pltpu.SMEM((64,), jnp.int32),
            pltpu.SMEM((1,), f32),
            pltpu.VMEM((CH,), f32),
            pltpu.VMEM((2, VW), f32),
            pltpu.VMEM((VW,), f32),
            pltpu.VMEM((9 * OUT_CH, 3 * CH), bf16),
            pltpu.VMEM((4 * CH, VW), bf16),
            pltpu.VMEM((VW, 3 * HD * LOCAL_HEADS), bf16),
            pltpu.VMEM((HD * LOCAL_HEADS, VW), bf16),
            pltpu.VMEM((512, CH), bf16),
            pltpu.VMEM((2 + CLIP_DEV, 16, 128), bf16),
            pltpu.VMEM((SP, 48, 128), bf16),
            pltpu.VMEM((6, ROWS, 128), f32),
            pltpu.VMEM((8, 15, ROWS, 128), f32),
            pltpu.VMEM((3, COLS, ROWS, 512), bf16),
            pltpu.VMEM((3, CELLS, CH), bf16),
            pltpu.VMEM((3, CELLS, CH), f32),
            pltpu.VMEM((CELLS, 3 * CH), bf16),
            pltpu.VMEM((SP, TOKENS, CH), bf16),
            pltpu.VMEM((SP, TOKENS, VW), f32),
            pltpu.VMEM((SP, TOKENS, VW), bf16),
            pltpu.VMEM((SP, TOKENS, CH), bf16),
            pltpu.VMEM((SP, TOKENS, CH), bf16),
            pltpu.VMEM((7, ROWS, 128), f32),
            pltpu.VMEM((SP, 48, 128), bf16),
            pltpu.VMEM((SP, 48, 128), bf16),
            pltpu.VMEM((15, 16, 128), f32),
            pltpu.VMEM((CLIP_DEV, 16, 128), bf16),
            pltpu.VMEM((8, 128), f32),
            pltpu.VMEM((3, COLS, ROWS, 512), f32),
            pltpu.SemaphoreType.DMA((11,)),
            pltpu.SemaphoreType.DMA((3, 9)),
            pltpu.SemaphoreType.DMA((4, SP)),
            pltpu.SemaphoreType.DMA((2, CLIP_DEV)),
            pltpu.SemaphoreType.DMA((2, CLIP_DEV)),
        ]
        + [pltpu.SemaphoreType.DMA((2, SP))] * 5,
        compiler_params=pltpu.CompilerParams(
            collective_id=0, has_side_effects=True, vmem_limit_bytes=60 * 1024 * 1024
        ),
        name="reward_step",
    )(
        latents,
        frame_list,
        reward_scale,
        norm_gain,
        conv_in_weight,
        ln_gain,
        head_vec,
        conv_weight.T,
        patch_weight,
        qkv_weight,
        out_weight,
    )
    reward, grad = pl.pallas_call(
        finish,
        out_shape=(
            jax.ShapeDtypeStruct((1, 1), f32),
            jax.ShapeDtypeStruct((FR_DEV, ROWS, 32), f32),
        ),
        in_specs=[vmem, vmem],
        out_specs=(vmem, vmem),
        name="finish",
    )(parts, rewards)
    return (reward.reshape(1), grad)


def solution(mesh):
    in_specs = (
        P("seq", None, "sp"),
        P(),
        P(),
        P(None, "sp"),
        P(),
        P("seq"),
        P(),
        P(),
        P(None, "sp"),
        P("sp", None),
        P(),
    )
    out_specs = (P("seq"), P("seq", None, "sp"))
    return jax.shard_map(body, mesh=mesh, in_specs=in_specs, out_specs=out_specs, check_vma=False)
```

```python
import functools

import jax
import jax.numpy as jnp
from jax import lax
from jax.experimental import pallas as pl
from jax.experimental.pallas import tpu as pltpu
from jax.sharding import PartitionSpec as P

LAT = 16
CH = 384
VW = 1024
HD = 64
COLS = 8
ROWS = 32
CLIP_FR = 16
FR_DEV = 2
CLIP_DEV = CLIP_FR // FR_DEV
SP = 4
OUT_CH = CH // SP
LOCAL_HEADS = 4
TOKENS = 64
CELLS = ROWS * COLS
HALF = 64
MESH = pl.DeviceIdType.MESH

norm_epsilon = 1e-06
layer_epsilon = 1e-05

f32 = jnp.float32
bf16 = jnp.bfloat16


def dot(left, right):
    return lax.dot_general(left, right, (((1,), (0,)), ((), ())), preferred_element_type=f32)


def dot_last(left, right):
    return lax.dot_general(left, right, (((1,), (1,)), ((), ())), preferred_element_type=f32)


def dot_first(left, right):
    return lax.dot_general(left, right, (((0,), (0,)), ((), ())), preferred_element_type=f32)


def iota(shape, dim):
    return lax.broadcasted_iota(jnp.int32, shape, dim)


def one_hot(condition):
    return jnp.where(condition, 1.0, 0.0).astype(bf16)


def row_mean(value):
    return jnp.sum(value, axis=-1, keepdims=True) * (1.0 / value.shape[-1])


def layer_stats(volume):
    center = row_mean(volume)
    moved = volume - center
    inverse = lax.rsqrt(row_mean(moved * moved) + layer_epsilon)
    return moved * inverse, inverse


def layer_back(whitened, inverse, scaled_grad):
    return inverse * (
        (scaled_grad - row_mean(scaled_grad)) - whitened * row_mean(scaled_grad * whitened)
    )


def shifted(value, offset):
    if offset == 0:
        return value
    blank = jnp.zeros(value.shape[:-2] + (1, value.shape[-1]), value.dtype)
    if offset > 0:
        return jnp.concatenate([value[..., 1:, :], blank], axis=-2)
    return jnp.concatenate([blank, value[..., :-1, :]], axis=-2)


def moved(value, offset):
    if offset == 0:
        return value
    blank = jnp.zeros((1,) + value.shape[1:], value.dtype)
    if offset > 0:
        return jnp.concatenate([value[1:], blank], axis=0)
    return jnp.concatenate([blank, value[:-1]], axis=0)


def start_copy(source, target, send, recv, device, pending):
    copy = pltpu.make_async_remote_copy(
        src_ref=source,
        dst_ref=target,
        send_sem=send,
        recv_sem=recv,
        device_id=device,
        device_id_type=MESH,
    )
    copy.start()
    pending.append(copy)
    return copy


def clip_partner(here, step):
    return (
        4 * lax.rem(here // 4 + step // 4, 2)
        + 2 * lax.rem(here // 2 + step // 2, 2)
        + lax.rem(here + step, 2)
    )


CLIP_STEPS = (6, 7, 4, 5, 2, 3, 1)


def exchange(pick, slots, sems, here, place, count, pending):
    copies = {}
    for step in sorted(range(1, count), key=lambda d: -min(d, count - d)):
        peer = lax.rem(here + step, count)
        copies[step] = start_copy(
            pick(step), slots.at[step], sems.at[0, step], sems.at[1, step], place(peer), pending
        )
    return copies


def wait_all(copies):
    for copy in copies.values():
        copy.wait_recv()


def kernel(
    lat_hbm,
    list_hbm,
    scale_hbm,
    gain_hbm,
    wi_hbm,
    ln_hbm,
    head_hbm,
    conv_hbm,
    patch_hbm,
    qkv_hbm,
    out_hbm,
    clip_in,
    reward_hbm,
    lat_ref,
    list_ref,
    scale_ref,
    gain_ref,
    ln_ref,
    head_ref,
    conv_ref,
    patch_ref,
    qkv_ref,
    out_ref,
    wi_pad,
    lat_seq,
    lat_sp,
    z_ref,
    rolled,
    cols,
    first,
    slope,
    lean,
    act,
    feat,
    embed,
    mix,
    patch_out,
    patch_in,
    lat_back,
    band_out,
    band_in,
    placed,
    clip_out,
    reward_ref,
    back_cols,
    swap,
    to_patch,
    from_patch,
    own_channels,
    load_sem,
    conv_sem,
    patch_sem,
    seq_sems,
    clip_sems,
    lat_sems,
    feat_sems,
    mix_sems,
    patch_sems,
    band_sems,
):
    seq = lax.axis_index("seq")
    sp = lax.axis_index("sp")
    local = lax.rem(seq, CLIP_DEV)
    base = seq - local

    def in_clip(peer):
        return (base + peer, sp)

    def in_band(peer):
        return (seq, peer)

    barrier = pltpu.get_barrier_semaphore()
    for step in range(1, CLIP_DEV):
        pl.semaphore_signal(
            barrier,
            inc=1,
            device_id=in_clip(lax.rem(local + step, CLIP_DEV)),
            device_id_type=MESH,
        )
    for step in range(1, SP):
        pl.semaphore_signal(
            barrier, inc=1, device_id=in_band(lax.rem(sp + step, SP)), device_id_type=MESH
        )

    loads = {}
    pending = []

    def load(name, source, target, sem):
        copy = pltpu.make_async_copy(source, target, sem)
        copy.start()
        loads.setdefault(name, []).append(copy)

    def loaded(*names):
        for name in names:
            for copy in loads.pop(name):
                copy.wait()

    for i, (name, source, target) in enumerate(
        (
            ("lat", lat_hbm, lat_ref),
            ("list", list_hbm, list_ref),
            ("gain", gain_hbm, gain_ref),
            ("wi", wi_hbm, wi_pad.at[0 : 27 * LAT]),
            ("ln", ln_hbm, ln_ref),
            ("head", head_hbm, head_ref),
            ("scale", scale_hbm, scale_ref),
        )
    ):
        load(name, source, target, load_sem.at[i])

    lat_seq[0:2] = jnp.zeros((2, 16, 128), bf16)
    loaded("lat")
    own = lat_ref[...].reshape(FR_DEV * ROWS, 32)
    packed = jnp.zeros((16, 128), f32)
    for j in range(4):
        spot = one_hot(iota((32, 128), 1) == iota((32, 128), 0) + 32 * j)
        packed = packed + dot(own[16 * j : 16 * j + 16], spot)
    lat_seq[pl.ds(2 + local, 1)] = packed.astype(bf16)[None]

    pl.semaphore_wait(barrier, CLIP_DEV - 1 + SP - 1)

    mine = lat_seq.at[pl.ds(2 + local, 1)]
    copies = {}
    for step in CLIP_STEPS:
        copies[step] = start_copy(
            mine,
            mine,
            seq_sems.at[0, step],
            seq_sems.at[1, step],
            in_clip(clip_partner(local, step)),
            pending,
        )

    for dt in range(3):
        for near in range(9):
            load(
                "conv",
                conv_hbm.at[:, CH * (9 * dt + near) : CH * (9 * dt + near + 1)],
                conv_ref.at[OUT_CH * near : OUT_CH * near + OUT_CH, CH * dt : CH * dt + CH],
                conv_sem.at[dt, near],
            )
    row, col = iota((512, 512), 0), iota((512, 512), 1)
    swap[...] = one_hot(
        ((row >> 7) == ((col >> 5) & 3)) & (((row >> 5) & 3) == (col >> 7)) & ((row & 31) == (col & 31))
    )
    wait_all(copies)

    loaded("list")
    where = lax.rem(list_ref[seq], CLIP_FR)
    chunk, odd = lax.div(where, 2), lax.rem(where, 2)
    lat_sp[pl.ds(sp, 1)] = lat_seq[pl.ds(chunk, 3)].reshape(1, 48, 128)
    copies = {}
    for step in (2, 1, 3):
        copies[step] = start_copy(
            lat_sp.at[sp],
            lat_sp.at[sp],
            lat_sems.at[0, step],
            lat_sems.at[1, step],
            in_band(lax.rem(sp + step, SP)),
            pending,
        )

    for k in range(4):
        for s in range(SP):
            load(
                "patch",
                patch_hbm.at[CH * k + OUT_CH * s : CH * k + OUT_CH * s + OUT_CH],
                patch_ref.at[CH * s + OUT_CH * k : CH * s + OUT_CH * k + OUT_CH],
                patch_sem.at[k, s],
            )
    load("qkv", qkv_hbm, qkv_ref, load_sem.at[7])
    load("out", out_hbm, out_ref, load_sem.at[8])
    wi_pad[27 * LAT :] = jnp.zeros((512 - 27 * LAT, CH), bf16)
    lat_back[...] = jnp.zeros(lat_back.shape, f32)
    placed[...] = jnp.zeros(placed.shape, f32)
    row, col = iota((256, 256), 0), iota((256, 256), 1)

    def cell_of(patch):
        kind, token = patch >> 6, patch & 63
        return (2 * (token >> 4) + (kind & 1)) * ROWS + 2 * (token & 15) + (kind >> 1)

    to_patch[...] = one_hot(col == cell_of(row))
    from_patch[...] = one_hot(row == cell_of(col))
    own_channels[...] = one_hot(iota((CH, OUT_CH), 0) == iota((CH, OUT_CH), 1) + sp * OUT_CH)
    loaded("gain", "wi", "conv")
    wait_all(copies)

    wide = jnp.concatenate([lat_sp[s] for s in range(SP)], axis=1)
    spots = dot(wide, swap[...])
    for c in range(3):
        for j in range(4):
            z_ref[2 * c + j // 2, 16 * (j % 2) : 16 * (j % 2) + 16] = spots[
                16 * c : 16 * c + 16, 128 * j : 128 * j + 128
            ]
    z = z_ref[pl.ds(odd, 5)]
    taps = jnp.stack([shifted(z, dr - 1) for dr in range(3)], axis=1).reshape(480, 128)
    for k in range(8):
        rolled[k] = (taps if k == 0 else pltpu.roll(taps, 16 * k, 1)).reshape(15, ROWS, 128)

    lane = iota((ROWS, 128), 1)
    pieces = []
    for block in range(4):
        inner = lax.rem(lane + 128 * block, 48) >> 4
        taps_here = [t for t in range(9) if 48 * t < 128 * block + 128 and 48 * t + 48 > 128 * block]
        pieces.append((inner, taps_here))

    def inside(inner, c):
        return ((inner > 0) | (c > 0)) & ((inner < 2) | (c < COLS - 1))

    def build(c, carry):
        for frame in range(3):
            for block, (inner, taps_here) in enumerate(pieces):
                value = None
                for tap in taps_here:
                    part = rolled[lax.rem(3 * tap + 9 - c, 8), 3 * frame + tap]
                    begin = 48 * tap - 128 * block
                    value = part if value is None else jnp.where(lane >= begin, part, value)
                cols[frame, c, :, 128 * block : 128 * block + 128] = jnp.where(
                    inside(inner, c), value, 0.0
                ).astype(bf16)
        return carry

    lax.fori_loop(0, COLS, build, 0, unroll=True)

    gain = gain_ref[...].reshape(1, CH)
    for frame in range(3):
        spots = dot(cols[frame].reshape(CELLS, 512), wi_pad[...])
        first[frame] = spots.astype(bf16)

    for frame in range(3):
        for half_frame in range(2):
            rows = slice(128 * half_frame, 128 * half_frame + 128)
            h = first[frame, rows].astype(f32)
            unit = h * lax.rsqrt(row_mean(h * h) + norm_epsilon) * gain
            act[rows, CH * frame : CH * frame + CH] = (unit * jax.nn.sigmoid(unit)).astype(bf16)

    spots = dot_last(act[...], conv_ref[...])
    total = dot(first[2], own_channels[...]).reshape(COLS, ROWS, OUT_CH)
    for dr in range(3):
        line = None
        for dc in range(3):
            start = OUT_CH * (3 * dr + dc)
            term = moved(spots[:, start : start + OUT_CH].reshape(COLS, ROWS, OUT_CH), dc - 1)
            line = term if line is None else line + term
        total = total + shifted(line, dr - 1)
    patches = dot(to_patch[...], total.reshape(CELLS, OUT_CH).astype(bf16))
    feat[0] = jnp.concatenate(
        [patches[TOKENS * k : TOKENS * k + TOKENS] for k in range(4)], axis=1
    ).astype(bf16)

    copies = exchange(
        lambda step: feat.at[0], feat, feat_sems, sp, in_band, SP, pending
    )
    loaded("patch")

    def embed_from(step):
        source = lax.rem(sp + SP - step, SP)
        rows = pl.ds(pl.multiple_of(source * CH, 128), CH)
        embed[pl.ds(source, 1)] = dot(feat[step], patch_ref[rows, :])[None]

    embed_from(0)
    for frame in range(3):
        h = first[frame].astype(f32)
        inverse = lax.rsqrt(row_mean(h * h) + norm_epsilon)
        lean[frame] = h * (inverse * inverse)
        unit = h * inverse * gain
        gate = jax.nn.sigmoid(unit)
        slope[frame] = gate * (1.0 + unit * (1.0 - gate)) * (gain * inverse)
    loaded("ln", "qkv", "out", "head", "scale")
    for step in (1, 3, 2):
        copies[step].wait_recv()
        embed_from(step)

    x = embed[0]
    for s in range(1, SP):
        x = x + embed[s]
    x = x.astype(bf16).astype(f32)
    white_in, inverse_in = layer_stats(x)
    gain_in, gain_out = ln_ref[0:1], ln_ref[1:2]
    qkv = dot((white_in * gain_in).astype(bf16), qkv_ref[...]).astype(bf16)
    heads = range(LOCAL_HEADS)

    def part_of(i):
        return [qkv[:, HD * (3 * h + i) : HD * (3 * h + i) + HD] for h in heads]

    def rows_of(stacked):
        return [stacked[TOKENS * h : TOKENS * h + TOKENS] for h in heads]

    query, key, value = part_of(0), part_of(1), part_of(2)
    scores = jnp.concatenate([dot_last(query[h], key[h]) for h in heads], axis=0) * (HD**-0.5)
    weights = jnp.exp(scores - jnp.max(scores, axis=-1, keepdims=True))
    probs = weights / jnp.sum(weights, axis=-1, keepdims=True)
    probs_low = rows_of(probs.astype(bf16))
    mixed = [dot(probs_low[h], value[h]).astype(bf16) for h in heads]
    mix[pl.ds(sp, 1)] = dot(jnp.concatenate(mixed, axis=1), out_ref[...]).astype(bf16)[None]

    copies = {}
    for step in (2, 1, 3):
        copies[step] = start_copy(
            mix.at[sp],
            mix.at[sp],
            mix_sems.at[0, step],
            mix_sems.at[1, step],
            in_band(lax.rem(sp + step, SP)),
            pending,
        )
    wait_all(copies)

    attended = mix[0].astype(f32)
    for s in range(1, SP):
        attended = attended + mix[s].astype(f32)
    y = x + attended
    white_out, inverse_out = layer_stats(y)
    vector = head_ref[...].reshape(1, VW)
    scaled = (scale_ref[0] * (1.0 / TOKENS)) * vector * gain_out
    dy = layer_back(white_out, inverse_out, scaled)
    do = dot_last(dy.astype(bf16), out_ref[...]).astype(bf16)
    d_out = [do[:, HD * h : HD * h + HD] for h in heads]
    d_probs = jnp.concatenate([dot_last(d_out[h], value[h]) for h in heads], axis=0)
    d_scores = probs * (d_probs - jnp.sum(d_probs * probs, axis=-1, keepdims=True)) * (HD**-0.5)
    d_scores = rows_of(d_scores.astype(bf16))
    grads = []
    for h in heads:
        grads.append(dot(d_scores[h], key[h]).astype(bf16))
        grads.append(dot_first(d_scores[h], query[h]).astype(bf16))
        grads.append(dot_first(probs_low[h], d_out[h]).astype(bf16))
    da = dot_last(jnp.concatenate(grads, axis=1), qkv_ref[...])
    dx = layer_back(white_in, inverse_in, da * gain_in) + dy * (1.0 / SP)
    dx_low = dx.astype(bf16)
    copies = {}
    for step in (2, 1, 3, 0):
        peer = lax.rem(sp + step, SP)
        rows = pl.ds(pl.multiple_of(peer * CH, 128), CH)
        block = dot_last(dx_low, patch_ref[rows, :]).astype(bf16)
        if step == 0:
            patch_in[0] = block
        else:
            patch_out[step] = block
            copies[step] = start_copy(
                patch_out.at[step],
                patch_in.at[step],
                patch_sems.at[0, step],
                patch_sems.at[1, step],
                in_band(peer),
                pending,
            )

    reward = jnp.sum(white_out * gain_out * vector, axis=1, keepdims=True)
    reward_ref[...] = jnp.broadcast_to(
        jnp.sum(reward, axis=0, keepdims=True) * (1.0 / TOKENS), (8, 128)
    )
    load("reward", reward_ref, reward_hbm, load_sem.at[9])

    wait_all(copies)

    summed = patch_in[0].astype(f32)
    for s in range(1, SP):
        summed = summed + patch_in[s].astype(f32)
    summed = jnp.concatenate(
        [summed[:, OUT_CH * k : OUT_CH * k + OUT_CH] for k in range(4)], axis=0
    )
    d_feat = dot(from_patch[...], summed.astype(bf16))
    d_cells = d_feat.reshape(COLS, ROWS, OUT_CH)
    lines = [shifted(d_cells, 1 - dr).astype(bf16) for dr in range(3)]
    spread_out = jnp.concatenate(
        [
            moved(lines[dr], 1 - dc).reshape(CELLS, OUT_CH)
            for dr in range(3)
            for dc in range(3)
        ],
        axis=1,
    )
    d_own = dot_last(d_feat.astype(bf16), own_channels[...])

    d_acts = dot(spread_out, conv_ref[...])
    for frame in (2, 1, 0):
        d_act = d_acts[:, CH * frame : CH * frame + CH]
        h = first[frame].astype(f32)
        d_unit = d_act * slope[frame]
        d_first = d_unit - lean[frame] * row_mean(d_unit * h)
        if frame == 2:
            d_first = d_first + d_own
        back_cols[frame] = dot_last(d_first.astype(bf16), wi_pad[...]).reshape(COLS, ROWS, 512)

    def collect(c, carry):
        totals = list(carry)
        for frame in range(3):
            for block, (inner, taps_here) in enumerate(pieces):
                value = jnp.where(
                    inside(inner, c), back_cols[frame, c, :, 128 * block : 128 * block + 128], 0.0
                )
                for tap in taps_here:
                    begin = 48 * tap - 128 * block
                    within = value
                    if begin > 0:
                        within = jnp.where(lane >= begin, within, 0.0)
                    if begin + 48 < 128:
                        within = jnp.where(lane < begin + 48, within, 0.0)
                    turn = lax.rem(16 * (c + 23 - 3 * tap + 8), 128)
                    totals[3 * frame + tap] = totals[3 * frame + tap] + pltpu.roll(within, turn, 1)
        return tuple(totals)

    gathered = lax.fori_loop(
        0, COLS, collect, tuple(jnp.zeros((ROWS, 128), f32) for _ in range(15)), unroll=True
    )
    gathered = jnp.stack(gathered, axis=0)
    gathered = gathered.reshape(5, 3, ROWS, 128)
    lat_back[1:6] = (
        gathered[:, 1] + shifted(gathered[:, 0], 1) + shifted(gathered[:, 2], -1)
    )
    aligned = lat_back[pl.ds(1 - odd, 6)].astype(bf16)
    wide = jnp.concatenate(
        [
            jnp.concatenate(
                [aligned[2 * c + j // 2, 16 * (j % 2) : 16 * (j % 2) + 16] for j in range(4)], axis=1
            )
            for c in range(3)
        ],
        axis=0,
    )
    bands = dot(wide, swap[...]).astype(bf16)
    for s in range(SP):
        band_out[s] = bands[:, 128 * s : 128 * s + 128]

    copies = exchange(
        lambda step: band_out.at[lax.rem(sp + step, SP)],
        band_in,
        band_sems,
        sp,
        in_band,
        SP,
        pending,
    )
    band_in[pl.ds(0, 1)] = band_out[pl.ds(sp, 1)]
    wait_all(copies)

    summed = band_in[0].astype(f32)
    for s in range(1, SP):
        summed = summed + band_in[s].astype(f32)
    placed[5:8] = summed.reshape(3, 16, 128)
    clip_out[...] = placed[pl.ds(7 - chunk, 8)].astype(bf16)
    copies = {}
    for step in CLIP_STEPS:
        peer = clip_partner(local, step)
        copies[step] = start_copy(
            clip_out.at[peer],
            clip_in.at[step],
            clip_sems.at[0, step],
            clip_sems.at[1, step],
            in_clip(peer),
            pending,
        )
    load("clip", clip_out.at[pl.ds(local, 1)], clip_in.at[0:1], load_sem.at[10])
    loaded("clip", "reward")
    for copy in pending[: 1 - CLIP_DEV]:
        copy.wait_send()
    wait_all(copies)

    for copy in pending[1 - CLIP_DEV :]:
        copy.wait_send()


def finish(clip_in, reward_in, reward_ref, grad_ref):
    summed = clip_in[0].astype(f32)
    for s in range(1, CLIP_DEV):
        summed = summed + clip_in[s].astype(f32)
    for j in range(4):
        grad_ref[j // 2, 16 * (j % 2) : 16 * (j % 2) + 16] = summed[:, 32 * j : 32 * j + 32]
    reward_ref[...] = reward_in[0:1, 0:1]


def body(
    latents,
    conv_in_weight,
    norm_gain,
    conv_weight,
    frame_list,
    reward_scale,
    patch_weight,
    ln_gain,
    qkv_weight,
    out_weight,
    head_vec,
):
    vmem = pl.BlockSpec(memory_space=pltpu.VMEM)
    hbm = pl.BlockSpec(memory_space=pltpu.HBM)
    parts, rewards = pl.pallas_call(
        kernel,
        out_shape=(
            jax.ShapeDtypeStruct((CLIP_DEV, 16, 128), bf16),
            jax.ShapeDtypeStruct((8, 128), f32),
        ),
        in_specs=[hbm] * 11,
        out_specs=(hbm, hbm),
        scratch_shapes=[
            pltpu.VMEM((FR_DEV, ROWS, 32), bf16),
            pltpu.SMEM((64,), jnp.int32),
            pltpu.SMEM((1,), f32),
            pltpu.VMEM((CH,), f32),
            pltpu.VMEM((2, VW), f32),
            pltpu.VMEM((VW,), f32),
            pltpu.VMEM((9 * OUT_CH, 3 * CH), bf16),
            pltpu.VMEM((4 * CH, VW), bf16),
            pltpu.VMEM((VW, 3 * HD * LOCAL_HEADS), bf16),
            pltpu.VMEM((HD * LOCAL_HEADS, VW), bf16),
            pltpu.VMEM((512, CH), bf16),
            pltpu.VMEM((2 + CLIP_DEV, 16, 128), bf16),
            pltpu.VMEM((SP, 48, 128), bf16),
            pltpu.VMEM((6, ROWS, 128), f32),
            pltpu.VMEM((8, 15, ROWS, 128), f32),
            pltpu.VMEM((3, COLS, ROWS, 512), bf16),
            pltpu.VMEM((3, CELLS, CH), bf16),
            pltpu.VMEM((3, CELLS, CH), f32),
            pltpu.VMEM((3, CELLS, CH), f32),
            pltpu.VMEM((CELLS, 3 * CH), bf16),
            pltpu.VMEM((SP, TOKENS, CH), bf16),
            pltpu.VMEM((SP, TOKENS, VW), f32),
            pltpu.VMEM((SP, TOKENS, VW), bf16),
            pltpu.VMEM((SP, TOKENS, CH), bf16),
            pltpu.VMEM((SP, TOKENS, CH), bf16),
            pltpu.VMEM((7, ROWS, 128), f32),
            pltpu.VMEM((SP, 48, 128), bf16),
            pltpu.VMEM((SP, 48, 128), bf16),
            pltpu.VMEM((15, 16, 128), f32),
            pltpu.VMEM((CLIP_DEV, 16, 128), bf16),
            pltpu.VMEM((8, 128), f32),
            pltpu.VMEM((3, COLS, ROWS, 512), f32),
            pltpu.VMEM((512, 512), bf16),
            pltpu.VMEM((CELLS, CELLS), bf16),
            pltpu.VMEM((CELLS, CELLS), bf16),
            pltpu.VMEM((CH, OUT_CH), bf16),
            pltpu.SemaphoreType.DMA((11,)),
            pltpu.SemaphoreType.DMA((3, 9)),
            pltpu.SemaphoreType.DMA((4, SP)),
            pltpu.SemaphoreType.DMA((2, CLIP_DEV)),
            pltpu.SemaphoreType.DMA((2, CLIP_DEV)),
        ]
        + [pltpu.SemaphoreType.DMA((2, SP))] * 5,
        compiler_params=pltpu.CompilerParams(
            collective_id=0, has_side_effects=True, vmem_limit_bytes=60 * 1024 * 1024
        ),
        name="reward_step",
    )(
        latents,
        frame_list,
        reward_scale,
        norm_gain,
        conv_in_weight,
        ln_gain,
        head_vec,
        conv_weight.T,
        patch_weight,
        qkv_weight,
        out_weight,
    )
    reward, grad = pl.pallas_call(
        finish,
        out_shape=(
            jax.ShapeDtypeStruct((1, 1), f32),
            jax.ShapeDtypeStruct((FR_DEV, ROWS, 32), f32),
        ),
        in_specs=[vmem, vmem],
        out_specs=(vmem, vmem),
        name="finish",
    )(parts, rewards)
    return (reward.reshape(1), grad)


def solution(mesh):
    in_specs = (
        P("seq", None, "sp"),
        P(),
        P(),
        P(None, "sp"),
        P(),
        P("seq"),
        P(),
        P(),
        P(None, "sp"),
        P("sp", None),
        P(),
    )
    out_specs = (P("seq"), P("seq", None, "sp"))
    return jax.shard_map(body, mesh=mesh, in_specs=in_specs, out_specs=out_specs, check_vma=False)
```

```python
import functools

import jax
import jax.numpy as jnp
from jax import lax
from jax.experimental import pallas as pl
from jax.experimental.pallas import tpu as pltpu
from jax.sharding import PartitionSpec as P

LAT = 16
CH = 384
VW = 1024
HD = 64
COLS = 8
ROWS = 32
CLIP_FR = 16
FR_DEV = 2
CLIP_DEV = CLIP_FR // FR_DEV
SP = 4
OUT_CH = CH // SP
LOCAL_HEADS = 4
TOKENS = 64
CELLS = ROWS * COLS
HALF = 64
MESH = pl.DeviceIdType.MESH

norm_epsilon = 1e-06
layer_epsilon = 1e-05

f32 = jnp.float32
bf16 = jnp.bfloat16


def dot(left, right):
    return lax.dot_general(left, right, (((1,), (0,)), ((), ())), preferred_element_type=f32)


def dot_last(left, right):
    return lax.dot_general(left, right, (((1,), (1,)), ((), ())), preferred_element_type=f32)


def dot_first(left, right):
    return lax.dot_general(left, right, (((0,), (0,)), ((), ())), preferred_element_type=f32)


def iota(shape, dim):
    return lax.broadcasted_iota(jnp.int32, shape, dim)


def one_hot(condition):
    return jnp.where(condition, 1.0, 0.0).astype(bf16)


def row_mean(value):
    return jnp.sum(value, axis=-1, keepdims=True) * (1.0 / value.shape[-1])


def layer_stats(volume):
    center = row_mean(volume)
    moved = volume - center
    inverse = lax.rsqrt(row_mean(moved * moved) + layer_epsilon)
    return moved * inverse, inverse


def layer_back(whitened, inverse, scaled_grad):
    return inverse * (
        (scaled_grad - row_mean(scaled_grad)) - whitened * row_mean(scaled_grad * whitened)
    )


def shifted(value, offset):
    if offset == 0:
        return value
    blank = jnp.zeros(value.shape[:-2] + (1, value.shape[-1]), value.dtype)
    if offset > 0:
        return jnp.concatenate([value[..., 1:, :], blank], axis=-2)
    return jnp.concatenate([blank, value[..., :-1, :]], axis=-2)


def moved(value, offset):
    if offset == 0:
        return value
    blank = jnp.zeros((1,) + value.shape[1:], value.dtype)
    if offset > 0:
        return jnp.concatenate([value[1:], blank], axis=0)
    return jnp.concatenate([blank, value[:-1]], axis=0)


def start_copy(source, target, send, recv, device, pending):
    copy = pltpu.make_async_remote_copy(
        src_ref=source,
        dst_ref=target,
        send_sem=send,
        recv_sem=recv,
        device_id=device,
        device_id_type=MESH,
    )
    copy.start()
    pending.append(copy)
    return copy


def clip_partner(here, step):
    return (
        4 * lax.rem(here // 4 + step // 4, 2)
        + 2 * lax.rem(here // 2 + step // 2, 2)
        + lax.rem(here + step, 2)
    )


CLIP_STEPS = (6, 7, 4, 5, 2, 3, 1)
ALL_STEPS = sorted(
    ((clip, band) for clip in range(CLIP_DEV) for band in range(SP) if clip or band),
    key=lambda step: -((0, 0, 1, 1, 2, 2, 2, 2)[step[0]] + (0, 1, 2, 1)[step[1]]),
)


def exchange(pick, slots, sems, here, place, count, pending):
    copies = {}
    for step in sorted(range(1, count), key=lambda d: -min(d, count - d)):
        peer = lax.rem(here + step, count)
        copies[step] = start_copy(
            pick(step), slots.at[step], sems.at[0, step], sems.at[1, step], place(peer), pending
        )
    return copies


def wait_all(copies):
    for copy in copies.values():
        copy.wait_recv()


def kernel(
    lat_hbm,
    list_hbm,
    scale_hbm,
    gain_hbm,
    wi_hbm,
    ln_hbm,
    head_hbm,
    conv_hbm,
    patch_hbm,
    qkv_hbm,
    out_hbm,
    clip_in,
    reward_hbm,
    lat_ref,
    list_ref,
    scale_ref,
    gain_ref,
    ln_ref,
    head_ref,
    conv_ref,
    patch_ref,
    qkv_ref,
    out_ref,
    wi_pad,
    lat_seq,
    lat_sp,
    z_ref,
    rolled,
    cols,
    first,
    slope,
    lean,
    act,
    feat,
    embed,
    mix,
    patch_out,
    patch_in,
    lat_back,
    placed,
    clip_out,
    reward_ref,
    back_cols,
    swap,
    to_patch,
    from_patch,
    own_channels,
    load_sem,
    conv_sem,
    patch_sem,
    seq_sems,
    clip_sems,
    lat_sems,
    feat_sems,
    mix_sems,
    patch_sems,
):
    seq = lax.axis_index("seq")
    sp = lax.axis_index("sp")
    local = lax.rem(seq, CLIP_DEV)
    base = seq - local

    def in_clip(peer):
        return (base + peer, sp)

    def in_band(peer):
        return (seq, peer)

    barrier = pltpu.get_barrier_semaphore()
    for step in range(1, CLIP_DEV):
        pl.semaphore_signal(
            barrier,
            inc=1,
            device_id=in_clip(lax.rem(local + step, CLIP_DEV)),
            device_id_type=MESH,
        )
    for step in range(1, SP):
        pl.semaphore_signal(
            barrier, inc=1, device_id=in_band(lax.rem(sp + step, SP)), device_id_type=MESH
        )

    loads = {}
    pending = []

    def load(name, source, target, sem):
        copy = pltpu.make_async_copy(source, target, sem)
        copy.start()
        loads.setdefault(name, []).append(copy)

    def loaded(*names):
        for name in names:
            for copy in loads.pop(name):
                copy.wait()

    for i, (name, source, target) in enumerate(
        (
            ("lat", lat_hbm, lat_ref),
            ("list", list_hbm, list_ref),
            ("gain", gain_hbm, gain_ref),
            ("wi", wi_hbm, wi_pad.at[0 : 27 * LAT]),
            ("ln", ln_hbm, ln_ref),
            ("head", head_hbm, head_ref),
            ("scale", scale_hbm, scale_ref),
        )
    ):
        load(name, source, target, load_sem.at[i])

    lat_seq[0:2] = jnp.zeros((2, 16, 128), bf16)
    loaded("lat")
    own = lat_ref[...].reshape(FR_DEV * ROWS, 32)
    packed = jnp.zeros((16, 128), f32)
    for j in range(4):
        spot = one_hot(iota((32, 128), 1) == iota((32, 128), 0) + 32 * j)
        packed = packed + dot(own[16 * j : 16 * j + 16], spot)
    lat_seq[pl.ds(2 + local, 1)] = packed.astype(bf16)[None]

    pl.semaphore_wait(barrier, CLIP_DEV - 1 + SP - 1)

    mine = lat_seq.at[pl.ds(2 + local, 1)]
    copies = {}
    for step in CLIP_STEPS:
        copies[step] = start_copy(
            mine,
            mine,
            seq_sems.at[0, step],
            seq_sems.at[1, step],
            in_clip(clip_partner(local, step)),
            pending,
        )

    for dt in range(3):
        for near in range(9):
            load(
                "conv",
                conv_hbm.at[:, CH * (9 * dt + near) : CH * (9 * dt + near + 1)],
                conv_ref.at[OUT_CH * near : OUT_CH * near + OUT_CH, CH * dt : CH * dt + CH],
                conv_sem.at[dt, near],
            )
    row, col = iota((512, 512), 0), iota((512, 512), 1)
    swap[...] = one_hot(
        ((row >> 7) == ((col >> 5) & 3)) & (((row >> 5) & 3) == (col >> 7)) & ((row & 31) == (col & 31))
    )
    wait_all(copies)

    loaded("list")
    where = lax.rem(list_ref[seq], CLIP_FR)
    chunk, odd = lax.div(where, 2), lax.rem(where, 2)
    lat_sp[pl.ds(sp, 1)] = lat_seq[pl.ds(chunk, 3)].reshape(1, 48, 128)
    copies = {}
    for step in (2, 1, 3):
        copies[step] = start_copy(
            lat_sp.at[sp],
            lat_sp.at[sp],
            lat_sems.at[0, step],
            lat_sems.at[1, step],
            in_band(lax.rem(sp + step, SP)),
            pending,
        )

    for k in range(4):
        for s in range(SP):
            load(
                "patch",
                patch_hbm.at[CH * k + OUT_CH * s : CH * k + OUT_CH * s + OUT_CH],
                patch_ref.at[CH * s + OUT_CH * k : CH * s + OUT_CH * k + OUT_CH],
                patch_sem.at[k, s],
            )
    load("qkv", qkv_hbm, qkv_ref, load_sem.at[7])
    load("out", out_hbm, out_ref, load_sem.at[8])
    wi_pad[27 * LAT :] = jnp.zeros((512 - 27 * LAT, CH), bf16)
    lat_back[...] = jnp.zeros(lat_back.shape, f32)
    placed[...] = jnp.zeros(placed.shape, bf16)
    row, col = iota((256, 256), 0), iota((256, 256), 1)

    def cell_of(patch):
        kind, token = patch >> 6, patch & 63
        return (2 * (token >> 4) + (kind & 1)) * ROWS + 2 * (token & 15) + (kind >> 1)

    to_patch[...] = one_hot(col == cell_of(row))
    from_patch[...] = one_hot(row == cell_of(col))
    own_channels[...] = one_hot(iota((CH, OUT_CH), 0) == iota((CH, OUT_CH), 1) + sp * OUT_CH)
    loaded("gain", "wi", "conv")
    wait_all(copies)

    wide = jnp.concatenate([lat_sp[s] for s in range(SP)], axis=1)
    spots = dot(wide, swap[...])
    for c in range(3):
        for j in range(4):
            z_ref[2 * c + j // 2, 16 * (j % 2) : 16 * (j % 2) + 16] = spots[
                16 * c : 16 * c + 16, 128 * j : 128 * j + 128
            ]
    z = z_ref[pl.ds(odd, 5)]
    taps = jnp.stack([shifted(z, dr - 1) for dr in range(3)], axis=1).reshape(480, 128)
    for k in range(8):
        rolled[k] = (taps if k == 0 else pltpu.roll(taps, 16 * k, 1)).reshape(15, ROWS, 128)

    lane = iota((ROWS, 128), 1)
    pieces = []
    for block in range(4):
        inner = lax.rem(lane + 128 * block, 48) >> 4
        taps_here = [t for t in range(9) if 48 * t < 128 * block + 128 and 48 * t + 48 > 128 * block]
        pieces.append((inner, taps_here))

    def inside(inner, c):
        return ((inner > 0) | (c > 0)) & ((inner < 2) | (c < COLS - 1))

    def build(c, carry):
        for frame in range(3):
            for block, (inner, taps_here) in enumerate(pieces):
                value = None
                for tap in taps_here:
                    part = rolled[lax.rem(3 * tap + 9 - c, 8), 3 * frame + tap]
                    begin = 48 * tap - 128 * block
                    value = part if value is None else jnp.where(lane >= begin, part, value)
                cols[frame, c, :, 128 * block : 128 * block + 128] = jnp.where(
                    inside(inner, c), value, 0.0
                ).astype(bf16)
        return carry

    lax.fori_loop(0, COLS, build, 0, unroll=True)

    gain = gain_ref[...].reshape(1, CH)
    for frame in range(3):
        spots = dot(cols[frame].reshape(CELLS, 512), wi_pad[...])
        first[frame] = spots.astype(bf16)

    for frame in range(3):
        for half_frame in range(2):
            rows = slice(128 * half_frame, 128 * half_frame + 128)
            h = first[frame, rows].astype(f32)
            unit = h * lax.rsqrt(row_mean(h * h) + norm_epsilon) * gain
            act[rows, CH * frame : CH * frame + CH] = (unit * jax.nn.sigmoid(unit)).astype(bf16)

    spots = dot_last(act[...], conv_ref[...])
    total = dot(first[2], own_channels[...]).reshape(COLS, ROWS, OUT_CH)
    for dr in range(3):
        line = None
        for dc in range(3):
            start = OUT_CH * (3 * dr + dc)
            term = moved(spots[:, start : start + OUT_CH].reshape(COLS, ROWS, OUT_CH), dc - 1)
            line = term if line is None else line + term
        total = total + shifted(line, dr - 1)
    patches = dot(to_patch[...], total.reshape(CELLS, OUT_CH).astype(bf16))
    feat[0] = jnp.concatenate(
        [patches[TOKENS * k : TOKENS * k + TOKENS] for k in range(4)], axis=1
    ).astype(bf16)

    copies = exchange(
        lambda step: feat.at[0], feat, feat_sems, sp, in_band, SP, pending
    )
    loaded("patch")

    def embed_from(step):
        source = lax.rem(sp + SP - step, SP)
        rows = pl.ds(pl.multiple_of(source * CH, 128), CH)
        embed[pl.ds(source, 1)] = dot(feat[step], patch_ref[rows, :])[None]

    embed_from(0)
    for frame in range(3):
        h = first[frame].astype(f32)
        inverse = lax.rsqrt(row_mean(h * h) + norm_epsilon)
        lean[frame] = h * (inverse * inverse)
        unit = h * inverse * gain
        gate = jax.nn.sigmoid(unit)
        slope[frame] = gate * (1.0 + unit * (1.0 - gate)) * (gain * inverse)
    loaded("ln", "qkv", "out", "head", "scale")
    for step in (1, 3, 2):
        copies[step].wait_recv()
        embed_from(step)

    x = embed[0]
    for s in range(1, SP):
        x = x + embed[s]
    x = x.astype(bf16).astype(f32)
    white_in, inverse_in = layer_stats(x)
    gain_in, gain_out = ln_ref[0:1], ln_ref[1:2]
    qkv = dot((white_in * gain_in).astype(bf16), qkv_ref[...]).astype(bf16)
    heads = range(LOCAL_HEADS)

    def part_of(i):
        return [qkv[:, HD * (3 * h + i) : HD * (3 * h + i) + HD] for h in heads]

    def rows_of(stacked):
        return [stacked[TOKENS * h : TOKENS * h + TOKENS] for h in heads]

    query, key, value = part_of(0), part_of(1), part_of(2)
    scores = jnp.concatenate([dot_last(query[h], key[h]) for h in heads], axis=0) * (HD**-0.5)
    weights = jnp.exp(scores - jnp.max(scores, axis=-1, keepdims=True))
    probs = weights / jnp.sum(weights, axis=-1, keepdims=True)
    probs_low = rows_of(probs.astype(bf16))
    mixed = [dot(probs_low[h], value[h]).astype(bf16) for h in heads]
    mix[pl.ds(sp, 1)] = dot(jnp.concatenate(mixed, axis=1), out_ref[...]).astype(bf16)[None]

    copies = {}
    for step in (2, 1, 3):
        copies[step] = start_copy(
            mix.at[sp],
            mix.at[sp],
            mix_sems.at[0, step],
            mix_sems.at[1, step],
            in_band(lax.rem(sp + step, SP)),
            pending,
        )
    wait_all(copies)

    attended = mix[0].astype(f32)
    for s in range(1, SP):
        attended = attended + mix[s].astype(f32)
    y = x + attended
    white_out, inverse_out = layer_stats(y)
    vector = head_ref[...].reshape(1, VW)
    scaled = (scale_ref[0] * (1.0 / TOKENS)) * vector * gain_out
    dy = layer_back(white_out, inverse_out, scaled)
    do = dot_last(dy.astype(bf16), out_ref[...]).astype(bf16)
    d_out = [do[:, HD * h : HD * h + HD] for h in heads]
    d_probs = jnp.concatenate([dot_last(d_out[h], value[h]) for h in heads], axis=0)
    d_scores = probs * (d_probs - jnp.sum(d_probs * probs, axis=-1, keepdims=True)) * (HD**-0.5)
    d_scores = rows_of(d_scores.astype(bf16))
    grads = []
    for h in heads:
        grads.append(dot(d_scores[h], key[h]).astype(bf16))
        grads.append(dot_first(d_scores[h], query[h]).astype(bf16))
        grads.append(dot_first(probs_low[h], d_out[h]).astype(bf16))
    da = dot_last(jnp.concatenate(grads, axis=1), qkv_ref[...])
    dx = layer_back(white_in, inverse_in, da * gain_in) + dy * (1.0 / SP)
    dx_low = dx.astype(bf16)
    copies = {}
    for step in (2, 1, 3, 0):
        peer = lax.rem(sp + step, SP)
        rows = pl.ds(pl.multiple_of(peer * CH, 128), CH)
        block = dot_last(dx_low, patch_ref[rows, :]).astype(bf16)
        if step == 0:
            patch_in[0] = block
        else:
            patch_out[step] = block
            copies[step] = start_copy(
                patch_out.at[step],
                patch_in.at[step],
                patch_sems.at[0, step],
                patch_sems.at[1, step],
                in_band(peer),
                pending,
            )

    reward = jnp.sum(white_out * gain_out * vector, axis=1, keepdims=True)
    reward_ref[...] = jnp.broadcast_to(
        jnp.sum(reward, axis=0, keepdims=True) * (1.0 / TOKENS), (8, 128)
    )
    load("reward", reward_ref, reward_hbm, load_sem.at[9])

    wait_all(copies)

    summed = patch_in[0].astype(f32)
    for s in range(1, SP):
        summed = summed + patch_in[s].astype(f32)
    summed = jnp.concatenate(
        [summed[:, OUT_CH * k : OUT_CH * k + OUT_CH] for k in range(4)], axis=0
    )
    d_feat = dot(from_patch[...], summed.astype(bf16))
    d_cells = d_feat.reshape(COLS, ROWS, OUT_CH)
    lines = [shifted(d_cells, 1 - dr).astype(bf16) for dr in range(3)]
    spread_out = jnp.concatenate(
        [
            moved(lines[dr], 1 - dc).reshape(CELLS, OUT_CH)
            for dr in range(3)
            for dc in range(3)
        ],
        axis=1,
    )
    d_own = dot_last(d_feat.astype(bf16), own_channels[...])

    d_acts = dot(spread_out, conv_ref[...])
    for frame in (2, 1, 0):
        d_act = d_acts[:, CH * frame : CH * frame + CH]
        h = first[frame].astype(f32)
        d_unit = d_act * slope[frame]
        d_first = d_unit - lean[frame] * row_mean(d_unit * h)
        if frame == 2:
            d_first = d_first + d_own
        back_cols[frame] = dot_last(d_first.astype(bf16), wi_pad[...]).reshape(COLS, ROWS, 512)

    def collect(c, carry):
        totals = list(carry)
        for frame in range(3):
            for block, (inner, taps_here) in enumerate(pieces):
                value = jnp.where(
                    inside(inner, c), back_cols[frame, c, :, 128 * block : 128 * block + 128], 0.0
                )
                for tap in taps_here:
                    begin = 48 * tap - 128 * block
                    within = value
                    if begin > 0:
                        within = jnp.where(lane >= begin, within, 0.0)
                    if begin + 48 < 128:
                        within = jnp.where(lane < begin + 48, within, 0.0)
                    turn = lax.rem(16 * (c + 23 - 3 * tap + 8), 128)
                    totals[3 * frame + tap] = totals[3 * frame + tap] + pltpu.roll(within, turn, 1)
        return tuple(totals)

    gathered = lax.fori_loop(
        0, COLS, collect, tuple(jnp.zeros((ROWS, 128), f32) for _ in range(15)), unroll=True
    )
    gathered = jnp.stack(gathered, axis=0)
    gathered = gathered.reshape(5, 3, ROWS, 128)
    lat_back[1:6] = (
        gathered[:, 1] + shifted(gathered[:, 0], 1) + shifted(gathered[:, 2], -1)
    )
    aligned = lat_back[pl.ds(1 - odd, 6)].astype(bf16)
    wide = jnp.concatenate(
        [
            jnp.concatenate(
                [aligned[2 * c + j // 2, 16 * (j % 2) : 16 * (j % 2) + 16] for j in range(4)], axis=1
            )
            for c in range(3)
        ],
        axis=0,
    )
    bands = dot(wide, swap[...]).astype(bf16)
    placed[5:8] = bands.reshape(3, 16, 512)
    ready = placed[pl.ds(7 - chunk, 8)]
    for s in range(SP):
        clip_out[s] = ready[:, :, 128 * s : 128 * s + 128]

    copies = {}
    for clip_step, band_step in ALL_STEPS:
        slot = SP * clip_step + band_step
        peer, band = clip_partner(local, clip_step), lax.rem(sp + band_step, SP)
        copies[slot] = start_copy(
            clip_out.at[band, peer],
            clip_in.at[slot],
            clip_sems.at[0, slot],
            clip_sems.at[1, slot],
            (base + peer, band),
            pending,
        )
    load("clip", clip_out.at[sp, local], clip_in.at[0], load_sem.at[10])
    loaded("clip", "reward")
    for copy in pending[: 1 - CLIP_DEV * SP]:
        copy.wait_send()
    wait_all(copies)

    for copy in pending[1 - CLIP_DEV * SP :]:
        copy.wait_send()


def finish(clip_in, reward_in, reward_ref, grad_ref):
    summed = clip_in[0].astype(f32)
    for s in range(1, CLIP_DEV * SP):
        summed = summed + clip_in[s].astype(f32)
    for j in range(4):
        grad_ref[j // 2, 16 * (j % 2) : 16 * (j % 2) + 16] = summed[:, 32 * j : 32 * j + 32]
    reward_ref[...] = reward_in[0:1, 0:1]


def body(
    latents,
    conv_in_weight,
    norm_gain,
    conv_weight,
    frame_list,
    reward_scale,
    patch_weight,
    ln_gain,
    qkv_weight,
    out_weight,
    head_vec,
):
    vmem = pl.BlockSpec(memory_space=pltpu.VMEM)
    hbm = pl.BlockSpec(memory_space=pltpu.HBM)
    parts, rewards = pl.pallas_call(
        kernel,
        out_shape=(
            jax.ShapeDtypeStruct((CLIP_DEV * SP, 16, 128), bf16),
            jax.ShapeDtypeStruct((8, 128), f32),
        ),
        in_specs=[hbm] * 11,
        out_specs=(hbm, hbm),
        scratch_shapes=[
            pltpu.VMEM((FR_DEV, ROWS, 32), bf16),
            pltpu.SMEM((64,), jnp.int32),
            pltpu.SMEM((1,), f32),
            pltpu.VMEM((CH,), f32),
            pltpu.VMEM((2, VW), f32),
            pltpu.VMEM((VW,), f32),
            pltpu.VMEM((9 * OUT_CH, 3 * CH), bf16),
            pltpu.VMEM((4 * CH, VW), bf16),
            pltpu.VMEM((VW, 3 * HD * LOCAL_HEADS), bf16),
            pltpu.VMEM((HD * LOCAL_HEADS, VW), bf16),
            pltpu.VMEM((512, CH), bf16),
            pltpu.VMEM((2 + CLIP_DEV, 16, 128), bf16),
            pltpu.VMEM((SP, 48, 128), bf16),
            pltpu.VMEM((6, ROWS, 128), f32),
            pltpu.VMEM((8, 15, ROWS, 128), f32),
            pltpu.VMEM((3, COLS, ROWS, 512), bf16),
            pltpu.VMEM((3, CELLS, CH), bf16),
            pltpu.VMEM((3, CELLS, CH), f32),
            pltpu.VMEM((3, CELLS, CH), f32),
            pltpu.VMEM((CELLS, 3 * CH), bf16),
            pltpu.VMEM((SP, TOKENS, CH), bf16),
            pltpu.VMEM((SP, TOKENS, VW), f32),
            pltpu.VMEM((SP, TOKENS, VW), bf16),
            pltpu.VMEM((SP, TOKENS, CH), bf16),
            pltpu.VMEM((SP, TOKENS, CH), bf16),
            pltpu.VMEM((7, ROWS, 128), f32),
            pltpu.VMEM((15, 16, 512), bf16),
            pltpu.VMEM((SP, CLIP_DEV, 16, 128), bf16),
            pltpu.VMEM((8, 128), f32),
            pltpu.VMEM((3, COLS, ROWS, 512), f32),
            pltpu.VMEM((512, 512), bf16),
            pltpu.VMEM((CELLS, CELLS), bf16),
            pltpu.VMEM((CELLS, CELLS), bf16),
            pltpu.VMEM((CH, OUT_CH), bf16),
            pltpu.SemaphoreType.DMA((11,)),
            pltpu.SemaphoreType.DMA((3, 9)),
            pltpu.SemaphoreType.DMA((4, SP)),
            pltpu.SemaphoreType.DMA((2, CLIP_DEV)),
            pltpu.SemaphoreType.DMA((2, CLIP_DEV * SP)),
        ]
        + [pltpu.SemaphoreType.DMA((2, SP))] * 4,
        compiler_params=pltpu.CompilerParams(
            collective_id=0, has_side_effects=True, vmem_limit_bytes=60 * 1024 * 1024
        ),
        name="reward_step",
    )(
        latents,
        frame_list,
        reward_scale,
        norm_gain,
        conv_in_weight,
        ln_gain,
        head_vec,
        conv_weight.T,
        patch_weight,
        qkv_weight,
        out_weight,
    )
    reward, grad = pl.pallas_call(
        finish,
        out_shape=(
            jax.ShapeDtypeStruct((1, 1), f32),
            jax.ShapeDtypeStruct((FR_DEV, ROWS, 32), f32),
        ),
        in_specs=[vmem, vmem],
        out_specs=(vmem, vmem),
        name="finish",
    )(parts, rewards)
    return (reward.reshape(1), grad)


def solution(mesh):
    in_specs = (
        P("seq", None, "sp"),
        P(),
        P(),
        P(None, "sp"),
        P(),
        P("seq"),
        P(),
        P(),
        P(None, "sp"),
        P("sp", None),
        P(),
    )
    out_specs = (P("seq"), P("seq", None, "sp"))
    return jax.shard_map(body, mesh=mesh, in_specs=in_specs, out_specs=out_specs, check_vma=False)
```

```python
import functools

import jax
import jax.numpy as jnp
from jax import lax
from jax.experimental import pallas as pl
from jax.experimental.pallas import tpu as pltpu
from jax.sharding import PartitionSpec as P

LAT = 16
CH = 384
VW = 1024
HD = 64
COLS = 8
ROWS = 32
CLIP_FR = 16
FR_DEV = 2
CLIP_DEV = CLIP_FR // FR_DEV
SP = 4
OUT_CH = CH // SP
LOCAL_HEADS = 4
TOKENS = 64
CELLS = ROWS * COLS
HALF = 64
MESH = pl.DeviceIdType.MESH

norm_epsilon = 1e-06
layer_epsilon = 1e-05

f32 = jnp.float32
bf16 = jnp.bfloat16


def dot(left, right):
    return lax.dot_general(left, right, (((1,), (0,)), ((), ())), preferred_element_type=f32)


def dot_last(left, right):
    return lax.dot_general(left, right, (((1,), (1,)), ((), ())), preferred_element_type=f32)


def dot_first(left, right):
    return lax.dot_general(left, right, (((0,), (0,)), ((), ())), preferred_element_type=f32)


def iota(shape, dim):
    return lax.broadcasted_iota(jnp.int32, shape, dim)


def one_hot(condition):
    return jnp.where(condition, 1.0, 0.0).astype(bf16)


def row_mean(value):
    return jnp.sum(value, axis=-1, keepdims=True) * (1.0 / value.shape[-1])


def layer_stats(volume):
    center = row_mean(volume)
    moved = volume - center
    inverse = lax.rsqrt(row_mean(moved * moved) + layer_epsilon)
    return moved * inverse, inverse


def layer_back(whitened, inverse, scaled_grad):
    return inverse * (
        (scaled_grad - row_mean(scaled_grad)) - whitened * row_mean(scaled_grad * whitened)
    )


def shifted(value, offset):
    if offset == 0:
        return value
    blank = jnp.zeros(value.shape[:-2] + (1, value.shape[-1]), value.dtype)
    if offset > 0:
        return jnp.concatenate([value[..., 1:, :], blank], axis=-2)
    return jnp.concatenate([blank, value[..., :-1, :]], axis=-2)


def moved(value, offset):
    if offset == 0:
        return value
    blank = jnp.zeros((1,) + value.shape[1:], value.dtype)
    if offset > 0:
        return jnp.concatenate([value[1:], blank], axis=0)
    return jnp.concatenate([blank, value[:-1]], axis=0)


def start_copy(source, target, send, recv, device, pending):
    copy = pltpu.make_async_remote_copy(
        src_ref=source,
        dst_ref=target,
        send_sem=send,
        recv_sem=recv,
        device_id=device,
        device_id_type=MESH,
    )
    copy.start()
    pending.append(copy)
    return copy


def clip_partner(here, step):
    return (
        4 * lax.rem(here // 4 + step // 4, 2)
        + 2 * lax.rem(here // 2 + step // 2, 2)
        + lax.rem(here + step, 2)
    )


CLIP_STEPS = (6, 7, 4, 5, 2, 3, 1)
ALL_STEPS = sorted(
    ((clip, band) for clip in range(CLIP_DEV) for band in range(SP) if clip or band),
    key=lambda step: -((0, 0, 1, 1, 2, 2, 2, 2)[step[0]] + (0, 1, 2, 1)[step[1]]),
)


def exchange(pick, slots, sems, here, place, count, pending):
    copies = {}
    for step in sorted(range(1, count), key=lambda d: -min(d, count - d)):
        peer = lax.rem(here + step, count)
        copies[step] = start_copy(
            pick(step), slots.at[step], sems.at[0, step], sems.at[1, step], place(peer), pending
        )
    return copies


def wait_all(copies):
    for copy in copies.values():
        copy.wait_recv()


def kernel(
    lat_hbm,
    list_hbm,
    scale_hbm,
    gain_hbm,
    wi_hbm,
    ln_hbm,
    head_hbm,
    conv_hbm,
    patch_hbm,
    qkv_hbm,
    out_hbm,
    clip_in,
    reward_hbm,
    lat_ref,
    list_ref,
    scale_ref,
    gain_ref,
    ln_ref,
    head_ref,
    conv_ref,
    patch_ref,
    qkv_ref,
    out_ref,
    wi_pad,
    lat_seq,
    lat_sp,
    z_ref,
    rolled,
    cols,
    first,
    slope,
    lean,
    act,
    feat,
    embed,
    mix,
    patch_out,
    patch_in,
    lat_back,
    placed,
    clip_out,
    reward_ref,
    back_cols,
    swap,
    to_patch,
    from_patch,
    own_channels,
    load_sem,
    conv_sem,
    patch_sem,
    seq_sems,
    clip_sems,
    lat_sems,
    feat_sems,
    mix_sems,
    patch_sems,
):
    seq = lax.axis_index("seq")
    sp = lax.axis_index("sp")
    local = lax.rem(seq, CLIP_DEV)
    base = seq - local

    def in_clip(peer):
        return (base + peer, sp)

    def in_band(peer):
        return (seq, peer)

    barrier = pltpu.get_barrier_semaphore()
    for step in range(1, CLIP_DEV):
        pl.semaphore_signal(
            barrier,
            inc=1,
            device_id=in_clip(lax.rem(local + step, CLIP_DEV)),
            device_id_type=MESH,
        )
    for step in range(1, SP):
        pl.semaphore_signal(
            barrier, inc=1, device_id=in_band(lax.rem(sp + step, SP)), device_id_type=MESH
        )

    loads = {}
    pending = []

    def load(name, source, target, sem):
        copy = pltpu.make_async_copy(source, target, sem)
        copy.start()
        loads.setdefault(name, []).append(copy)

    def loaded(*names):
        for name in names:
            for copy in loads.pop(name):
                copy.wait()

    for i, (name, source, target) in enumerate(
        (
            ("lat", lat_hbm, lat_ref),
            ("list", list_hbm, list_ref),
            ("gain", gain_hbm, gain_ref),
            ("wi", wi_hbm, wi_pad.at[0 : 27 * LAT]),
            ("ln", ln_hbm, ln_ref),
            ("head", head_hbm, head_ref),
            ("scale", scale_hbm, scale_ref),
        )
    ):
        load(name, source, target, load_sem.at[i])

    lat_seq[0:2] = jnp.zeros((2, 16, 128), bf16)
    loaded("lat")
    own = lat_ref[...].reshape(FR_DEV * ROWS, 32)
    packed = jnp.zeros((16, 128), f32)
    for j in range(4):
        spot = one_hot(iota((32, 128), 1) == iota((32, 128), 0) + 32 * j)
        packed = packed + dot(own[16 * j : 16 * j + 16], spot)
    lat_seq[pl.ds(2 + local, 1)] = packed.astype(bf16)[None]

    pl.semaphore_wait(barrier, CLIP_DEV - 1 + SP - 1)

    mine = lat_seq.at[pl.ds(2 + local, 1)]
    copies = {}
    for step in CLIP_STEPS:
        copies[step] = start_copy(
            mine,
            mine,
            seq_sems.at[0, step],
            seq_sems.at[1, step],
            in_clip(clip_partner(local, step)),
            pending,
        )

    for dt in range(3):
        for near in range(9):
            load(
                "conv",
                conv_hbm.at[:, CH * (9 * dt + near) : CH * (9 * dt + near + 1)],
                conv_ref.at[OUT_CH * near : OUT_CH * near + OUT_CH, CH * dt : CH * dt + CH],
                conv_sem.at[dt, near],
            )
    row, col = iota((512, 512), 0), iota((512, 512), 1)
    swap[...] = one_hot(
        ((row >> 7) == ((col >> 5) & 3)) & (((row >> 5) & 3) == (col >> 7)) & ((row & 31) == (col & 31))
    )
    loaded("list")
    where = lax.rem(list_ref[seq], CLIP_FR)
    chunk, odd = lax.div(where, 2), lax.rem(where, 2)
    wait_all(copies)

    lat_sp[pl.ds(sp, 1)] = lat_seq[pl.ds(chunk, 3)].reshape(1, 48, 128)
    copies = {}
    for step in (2, 1, 3):
        copies[step] = start_copy(
            lat_sp.at[sp],
            lat_sp.at[sp],
            lat_sems.at[0, step],
            lat_sems.at[1, step],
            in_band(lax.rem(sp + step, SP)),
            pending,
        )

    for k in range(4):
        for s in range(SP):
            load(
                "patch",
                patch_hbm.at[CH * k + OUT_CH * s : CH * k + OUT_CH * s + OUT_CH],
                patch_ref.at[CH * s + OUT_CH * k : CH * s + OUT_CH * k + OUT_CH],
                patch_sem.at[k, s],
            )
    load("qkv", qkv_hbm, qkv_ref, load_sem.at[7])
    load("out", out_hbm, out_ref, load_sem.at[8])
    wi_pad[27 * LAT :] = jnp.zeros((512 - 27 * LAT, CH), bf16)
    lat_back[...] = jnp.zeros(lat_back.shape, f32)
    placed[...] = jnp.zeros(placed.shape, bf16)
    row, col = iota((256, 256), 0), iota((256, 256), 1)

    def cell_of(patch):
        kind, token = patch >> 6, patch & 63
        return (2 * (token >> 4) + (kind & 1)) * ROWS + 2 * (token & 15) + (kind >> 1)

    to_patch[...] = one_hot(col == cell_of(row))
    from_patch[...] = one_hot(row == cell_of(col))
    own_channels[...] = one_hot(iota((CH, OUT_CH), 0) == iota((CH, OUT_CH), 1) + sp * OUT_CH)
    loaded("gain", "wi", "conv")
    wait_all(copies)

    wide = jnp.concatenate([lat_sp[s] for s in range(SP)], axis=1)
    spots = dot(wide, swap[...])
    for c in range(3):
        for j in range(4):
            z_ref[2 * c + j // 2, 16 * (j % 2) : 16 * (j % 2) + 16] = spots[
                16 * c : 16 * c + 16, 128 * j : 128 * j + 128
            ]
    z = z_ref[pl.ds(odd, 5)]
    taps = jnp.stack([shifted(z, dr - 1) for dr in range(3)], axis=1).reshape(480, 128)
    for k in range(8):
        rolled[k] = (taps if k == 0 else pltpu.roll(taps, 16 * k, 1)).reshape(15, ROWS, 128)

    lane = iota((ROWS, 128), 1)
    pieces = []
    for block in range(4):
        inner = lax.rem(lane + 128 * block, 48) >> 4
        taps_here = [t for t in range(9) if 48 * t < 128 * block + 128 and 48 * t + 48 > 128 * block]
        pieces.append((inner, taps_here))

    def inside(inner, c):
        return ((inner > 0) | (c > 0)) & ((inner < 2) | (c < COLS - 1))

    def build(c, carry):
        for frame in range(3):
            for block, (inner, taps_here) in enumerate(pieces):
                value = None
                for tap in taps_here:
                    part = rolled[lax.rem(3 * tap + 9 - c, 8), 3 * frame + tap]
                    begin = 48 * tap - 128 * block
                    value = part if value is None else jnp.where(lane >= begin, part, value)
                cols[frame, c, :, 128 * block : 128 * block + 128] = jnp.where(
                    inside(inner, c), value, 0.0
                ).astype(bf16)
        return carry

    lax.fori_loop(0, COLS, build, 0, unroll=True)

    gain = gain_ref[...].reshape(1, CH)
    for frame in range(3):
        spots = dot(cols[frame].reshape(CELLS, 512), wi_pad[...])
        first[frame] = spots.astype(bf16)

    for frame in range(3):
        for half_frame in range(2):
            rows = slice(128 * half_frame, 128 * half_frame + 128)
            h = first[frame, rows].astype(f32)
            unit = h * lax.rsqrt(row_mean(h * h) + norm_epsilon) * gain
            act[rows, CH * frame : CH * frame + CH] = (unit * jax.nn.sigmoid(unit)).astype(bf16)

    spots = dot_last(act[...], conv_ref[...])
    total = dot(first[2], own_channels[...]).reshape(COLS, ROWS, OUT_CH)
    for dr in range(3):
        line = None
        for dc in range(3):
            start = OUT_CH * (3 * dr + dc)
            term = moved(spots[:, start : start + OUT_CH].reshape(COLS, ROWS, OUT_CH), dc - 1)
            line = term if line is None else line + term
        total = total + shifted(line, dr - 1)
    patches = dot(to_patch[...], total.reshape(CELLS, OUT_CH).astype(bf16))
    feat[0] = jnp.concatenate(
        [patches[TOKENS * k : TOKENS * k + TOKENS] for k in range(4)], axis=1
    ).astype(bf16)

    copies = exchange(
        lambda step: feat.at[0], feat, feat_sems, sp, in_band, SP, pending
    )
    loaded("patch")

    def embed_from(step):
        source = lax.rem(sp + SP - step, SP)
        rows = pl.ds(pl.multiple_of(source * CH, 128), CH)
        embed[pl.ds(source, 1)] = dot(feat[step], patch_ref[rows, :])[None]

    embed_from(0)
    for frame in range(3):
        h = first[frame].astype(f32)
        inverse = lax.rsqrt(row_mean(h * h) + norm_epsilon)
        lean[frame] = h * (inverse * inverse)
        unit = h * inverse * gain
        gate = jax.nn.sigmoid(unit)
        slope[frame] = gate * (1.0 + unit * (1.0 - gate)) * (gain * inverse)
    loaded("ln", "qkv", "out", "head", "scale")
    for step in (1, 3, 2):
        copies[step].wait_recv()
        embed_from(step)

    x = embed[0]
    for s in range(1, SP):
        x = x + embed[s]
    x = x.astype(bf16).astype(f32)
    white_in, inverse_in = layer_stats(x)
    gain_in, gain_out = ln_ref[0:1], ln_ref[1:2]
    qkv = dot((white_in * gain_in).astype(bf16), qkv_ref[...]).astype(bf16)
    heads = range(LOCAL_HEADS)

    def part_of(i):
        return [qkv[:, HD * (3 * h + i) : HD * (3 * h + i) + HD] for h in heads]

    def rows_of(stacked):
        return [stacked[TOKENS * h : TOKENS * h + TOKENS] for h in heads]

    query, key, value = part_of(0), part_of(1), part_of(2)
    scores = jnp.concatenate([dot_last(query[h], key[h]) for h in heads], axis=0) * (HD**-0.5)
    weights = jnp.exp(scores - jnp.max(scores, axis=-1, keepdims=True))
    probs = weights * (1.0 / jnp.sum(weights, axis=-1, keepdims=True))
    probs_low = rows_of(probs.astype(bf16))
    mixed = [dot(probs_low[h], value[h]).astype(bf16) for h in heads]
    mix[pl.ds(sp, 1)] = dot(jnp.concatenate(mixed, axis=1), out_ref[...]).astype(bf16)[None]

    copies = {}
    for step in (2, 1, 3):
        copies[step] = start_copy(
            mix.at[sp],
            mix.at[sp],
            mix_sems.at[0, step],
            mix_sems.at[1, step],
            in_band(lax.rem(sp + step, SP)),
            pending,
        )
    wait_all(copies)

    attended = mix[0].astype(f32)
    for s in range(1, SP):
        attended = attended + mix[s].astype(f32)
    y = x + attended
    white_out, inverse_out = layer_stats(y)
    vector = head_ref[...].reshape(1, VW)
    scaled = (scale_ref[0] * (1.0 / TOKENS)) * vector * gain_out
    dy = layer_back(white_out, inverse_out, scaled)
    do = dot_last(dy.astype(bf16), out_ref[...]).astype(bf16)
    d_out = [do[:, HD * h : HD * h + HD] for h in heads]
    d_probs = jnp.concatenate([dot_last(d_out[h], value[h]) for h in heads], axis=0)
    d_scores = probs * (d_probs - jnp.sum(d_probs * probs, axis=-1, keepdims=True)) * (HD**-0.5)
    d_scores = rows_of(d_scores.astype(bf16))
    grads = []
    for h in heads:
        grads.append(dot(d_scores[h], key[h]).astype(bf16))
        grads.append(dot_first(d_scores[h], query[h]).astype(bf16))
        grads.append(dot_first(probs_low[h], d_out[h]).astype(bf16))
    da = dot_last(jnp.concatenate(grads, axis=1), qkv_ref[...])
    dx = layer_back(white_in, inverse_in, da * gain_in) + dy * (1.0 / SP)
    dx_low = dx.astype(bf16)
    copies = {}
    for step in (2, 1, 3, 0):
        peer = lax.rem(sp + step, SP)
        rows = pl.ds(pl.multiple_of(peer * CH, 128), CH)
        block = dot_last(dx_low, patch_ref[rows, :]).astype(bf16)
        if step == 0:
            patch_in[0] = block
        else:
            patch_out[step] = block
            copies[step] = start_copy(
                patch_out.at[step],
                patch_in.at[step],
                patch_sems.at[0, step],
                patch_sems.at[1, step],
                in_band(peer),
                pending,
            )

    reward = jnp.sum(white_out * gain_out * vector, axis=1, keepdims=True)
    reward_ref[...] = jnp.broadcast_to(
        jnp.sum(reward, axis=0, keepdims=True) * (1.0 / TOKENS), (8, 128)
    )
    load("reward", reward_ref, reward_hbm, load_sem.at[9])

    summed = patch_in[0].astype(f32)
    for step in (1, 3, 2):
        copies[step].wait_recv()
        summed = summed + patch_in[step].astype(f32)

    summed = jnp.concatenate(
        [summed[:, OUT_CH * k : OUT_CH * k + OUT_CH] for k in range(4)], axis=0
    )
    d_feat = dot(from_patch[...], summed.astype(bf16))
    d_cells = d_feat.reshape(COLS, ROWS, OUT_CH)
    lines = [shifted(d_cells, 1 - dr).astype(bf16) for dr in range(3)]
    spread_out = jnp.concatenate(
        [
            moved(lines[dr], 1 - dc).reshape(CELLS, OUT_CH)
            for dr in range(3)
            for dc in range(3)
        ],
        axis=1,
    )
    d_own = dot_last(d_feat.astype(bf16), own_channels[...])

    d_acts = dot(spread_out, conv_ref[...])
    for frame in (2, 1, 0):
        d_act = d_acts[:, CH * frame : CH * frame + CH]
        h = first[frame].astype(f32)
        d_unit = d_act * slope[frame]
        d_first = d_unit - lean[frame] * row_mean(d_unit * h)
        if frame == 2:
            d_first = d_first + d_own
        back_cols[frame] = dot_last(d_first.astype(bf16), wi_pad[...]).reshape(COLS, ROWS, 512)

    def collect(c, carry):
        totals = list(carry)
        for frame in range(3):
            for block, (inner, taps_here) in enumerate(pieces):
                value = jnp.where(
                    inside(inner, c), back_cols[frame, c, :, 128 * block : 128 * block + 128], 0.0
                )
                for tap in taps_here:
                    begin = 48 * tap - 128 * block
                    within = value
                    if begin > 0:
                        within = jnp.where(lane >= begin, within, 0.0)
                    if begin + 48 < 128:
                        within = jnp.where(lane < begin + 48, within, 0.0)
                    turn = lax.rem(16 * (c + 23 - 3 * tap + 8), 128)
                    totals[3 * frame + tap] = totals[3 * frame + tap] + pltpu.roll(within, turn, 1)
        return tuple(totals)

    gathered = lax.fori_loop(
        0, COLS, collect, tuple(jnp.zeros((ROWS, 128), f32) for _ in range(15)), unroll=True
    )
    gathered = jnp.stack(gathered, axis=0)
    gathered = gathered.reshape(5, 3, ROWS, 128)
    lat_back[1:6] = (
        gathered[:, 1] + shifted(gathered[:, 0], 1) + shifted(gathered[:, 2], -1)
    )
    aligned = lat_back[pl.ds(1 - odd, 6)].astype(bf16)
    wide = jnp.concatenate(
        [
            jnp.concatenate(
                [aligned[2 * c + j // 2, 16 * (j % 2) : 16 * (j % 2) + 16] for j in range(4)], axis=1
            )
            for c in range(3)
        ],
        axis=0,
    )
    bands = dot(wide, swap[...]).astype(bf16)
    placed[5:8] = bands.reshape(3, 16, 512)
    ready = placed[pl.ds(7 - chunk, 8)]
    for s in range(SP):
        clip_out[s] = ready[:, :, 128 * s : 128 * s + 128]

    copies = {}
    for clip_step, band_step in ALL_STEPS:
        slot = SP * clip_step + band_step
        peer, band = clip_partner(local, clip_step), lax.rem(sp + band_step, SP)
        copies[slot] = start_copy(
            clip_out.at[band, peer],
            clip_in.at[slot],
            clip_sems.at[0, slot],
            clip_sems.at[1, slot],
            (base + peer, band),
            pending,
        )
    load("clip", clip_out.at[sp, local], clip_in.at[0], load_sem.at[10])
    loaded("clip", "reward")
    for copy in pending[: 1 - CLIP_DEV * SP]:
        copy.wait_send()
    wait_all(copies)

    for copy in pending[1 - CLIP_DEV * SP :]:
        copy.wait_send()


def finish(clip_in, reward_in, reward_ref, grad_ref):
    summed = clip_in[0].astype(f32)
    for s in range(1, CLIP_DEV * SP):
        summed = summed + clip_in[s].astype(f32)
    for j in range(4):
        grad_ref[j // 2, 16 * (j % 2) : 16 * (j % 2) + 16] = summed[:, 32 * j : 32 * j + 32]
    reward_ref[...] = reward_in[0:1, 0:1]


def body(
    latents,
    conv_in_weight,
    norm_gain,
    conv_weight,
    frame_list,
    reward_scale,
    patch_weight,
    ln_gain,
    qkv_weight,
    out_weight,
    head_vec,
):
    vmem = pl.BlockSpec(memory_space=pltpu.VMEM)
    hbm = pl.BlockSpec(memory_space=pltpu.HBM)
    parts, rewards = pl.pallas_call(
        kernel,
        out_shape=(
            jax.ShapeDtypeStruct((CLIP_DEV * SP, 16, 128), bf16),
            jax.ShapeDtypeStruct((8, 128), f32),
        ),
        in_specs=[hbm] * 11,
        out_specs=(hbm, hbm),
        scratch_shapes=[
            pltpu.VMEM((FR_DEV, ROWS, 32), bf16),
            pltpu.SMEM((64,), jnp.int32),
            pltpu.SMEM((1,), f32),
            pltpu.VMEM((CH,), f32),
            pltpu.VMEM((2, VW), f32),
            pltpu.VMEM((VW,), f32),
            pltpu.VMEM((9 * OUT_CH, 3 * CH), bf16),
            pltpu.VMEM((4 * CH, VW), bf16),
            pltpu.VMEM((VW, 3 * HD * LOCAL_HEADS), bf16),
            pltpu.VMEM((HD * LOCAL_HEADS, VW), bf16),
            pltpu.VMEM((512, CH), bf16),
            pltpu.VMEM((2 + CLIP_DEV, 16, 128), bf16),
            pltpu.VMEM((SP, 48, 128), bf16),
            pltpu.VMEM((6, ROWS, 128), f32),
            pltpu.VMEM((8, 15, ROWS, 128), f32),
            pltpu.VMEM((3, COLS, ROWS, 512), bf16),
            pltpu.VMEM((3, CELLS, CH), bf16),
            pltpu.VMEM((3, CELLS, CH), f32),
            pltpu.VMEM((3, CELLS, CH), f32),
            pltpu.VMEM((CELLS, 3 * CH), bf16),
            pltpu.VMEM((SP, TOKENS, CH), bf16),
            pltpu.VMEM((SP, TOKENS, VW), f32),
            pltpu.VMEM((SP, TOKENS, VW), bf16),
            pltpu.VMEM((SP, TOKENS, CH), bf16),
            pltpu.VMEM((SP, TOKENS, CH), bf16),
            pltpu.VMEM((7, ROWS, 128), f32),
            pltpu.VMEM((15, 16, 512), bf16),
            pltpu.VMEM((SP, CLIP_DEV, 16, 128), bf16),
            pltpu.VMEM((8, 128), f32),
            pltpu.VMEM((3, COLS, ROWS, 512), f32),
            pltpu.VMEM((512, 512), bf16),
            pltpu.VMEM((CELLS, CELLS), bf16),
            pltpu.VMEM((CELLS, CELLS), bf16),
            pltpu.VMEM((CH, OUT_CH), bf16),
            pltpu.SemaphoreType.DMA((11,)),
            pltpu.SemaphoreType.DMA((3, 9)),
            pltpu.SemaphoreType.DMA((4, SP)),
            pltpu.SemaphoreType.DMA((2, CLIP_DEV)),
            pltpu.SemaphoreType.DMA((2, CLIP_DEV * SP)),
        ]
        + [pltpu.SemaphoreType.DMA((2, SP))] * 4,
        compiler_params=pltpu.CompilerParams(
            collective_id=0, has_side_effects=True, vmem_limit_bytes=60 * 1024 * 1024
        ),
        name="reward_step",
    )(
        latents,
        frame_list,
        reward_scale,
        norm_gain,
        conv_in_weight,
        ln_gain,
        head_vec,
        conv_weight.T,
        patch_weight,
        qkv_weight,
        out_weight,
    )
    reward, grad = pl.pallas_call(
        finish,
        out_shape=(
            jax.ShapeDtypeStruct((1, 1), f32),
            jax.ShapeDtypeStruct((FR_DEV, ROWS, 32), f32),
        ),
        in_specs=[vmem, vmem],
        out_specs=(vmem, vmem),
        name="finish",
    )(parts, rewards)
    return (reward.reshape(1), grad)


def solution(mesh):
    in_specs = (
        P("seq", None, "sp"),
        P(),
        P(),
        P(None, "sp"),
        P(),
        P("seq"),
        P(),
        P(),
        P(None, "sp"),
        P("sp", None),
        P(),
    )
    out_specs = (P("seq"), P("seq", None, "sp"))
    return jax.shard_map(body, mesh=mesh, in_specs=in_specs, out_specs=out_specs, check_vma=False)
```
